256 devices in a mesh: col: 32 (over x, z), row: 8 (over y, core).
Axes of the slice: x: 4, y: 4, z: 8, core: 2. Of those that a mesh axis runs over, the one named last changes fastest.
Arguments:
- matrix: float32 [8192, 8192], P('row', 'col'), as said below
- flips: int32 [4, 32], P(None, 'col'), may hold values 0 or 1
Outputs:
- rotated: float32 [8192, 8192], P('row', 'col')
The draws below stay inside these ranges and needn't reach their ends.
Inputs may be any that keep to these rules, and one draw needn't show every extreme that they name: `matrix`: dense real-valued activations.
All inputs are finite; a program needn't handle non-finite values. No bound on the sum of `flips` on one device may be relied on, other than what follows from the above.
Results may differ from the reference program's by a relative error of at most 0.0003.
Values sent between devices are 32-bit elements; how exact they have to be, the bound alone decides.
A program may use at most 64 MiB of HBM per device.

```python
import math
import jax
import jax.numpy as jnp
from jax import lax

BLOCK = 128
ROUNDS = 4
STEPS = 8
PAIRS = 32
ROWS = 8192
COLS = 8192


def draw_matrix(key, part):
    key = jax.random.fold_in(key, 11)
    first, second = jax.random.split(key, 2)
    col_scale = jnp.exp(jax.random.uniform(second, (1, COLS), jnp.float32, math.log(0.1), math.log(10.0)))
    values = jax.random.normal(first, (ROWS, COLS), jnp.float32) * col_scale
    return values.astype(jnp.float32)


def set_ends(drawn, rng, low, high):
    index_at = [jax.random.randint(jax.random.fold_in(rng, axis), (), 0, length) for axis, length in enumerate(drawn.shape)]
    main_axis = drawn.shape.index(max(drawn.shape))
    beside = index_at[:main_axis] + [(index_at[main_axis] + 1) % drawn.shape[main_axis]] + index_at[main_axis + 1:]
    return drawn.at[tuple(index_at)].set(low).at[tuple(beside)].set(high)


def setup_inputs(seed: int = 0) -> dict:
    key_list = jax.random.split(jax.random.key(seed), 3)
    matrix = draw_matrix(jax.random.fold_in(key_list[2], 71), 0)
    flips = set_ends((jax.random.randint(key_list[1], (ROUNDS, PAIRS), 0, 2) < 1).astype(jnp.int32), jax.random.fold_in(key_list[1], 1), 0, 1)
    return {"matrix": matrix, "flips": flips}


HIGH = lax.Precision.HIGHEST

def reorder_columns(values, width):
    return jnp.concatenate([values[:, 0:1], values[:, width:width + 1], values[:, 1:width - 1], values[:, width + 1:], values[:, width - 1:width]], axis=1)

def reorder_rows(values, width):
    return jnp.concatenate([values[0:1], values[width:width + 1], values[1:width - 1], values[width + 1:], values[width - 1:width]], axis=0)

def turn_pair(gram, basis):
    width = gram.shape[0] // 2
    diagonal_now = jnp.diagonal(gram)
    first = diagonal_now[:width]
    second = diagonal_now[width:]
    cross = jnp.diagonal(gram[:width, width:])
    differ = second - first
    sign_part = jnp.where(differ >= 0, 1.0, -1.0)
    tangent = 2.0 * cross * sign_part / (jnp.abs(differ) + jnp.sqrt(differ * differ + 4.0 * cross * cross) + 1e-06 * (first + second))
    cosine = 1.0 / jnp.sqrt(1.0 + tangent * tangent)
    sine_term = cosine * tangent

    def columns(values):
        leading = values[:, :width]
        trailing = values[:, width:]
        return jnp.concatenate([leading * cosine - trailing * sine_term, leading * sine_term + trailing * cosine], axis=1)
    gram = columns(gram)
    leading = gram[:width]
    trailing = gram[width:]
    gram = jnp.concatenate([leading * cosine[:, None] - trailing * sine_term[:, None], leading * sine_term[:, None] + trailing * cosine[:, None]], axis=0)
    basis = columns(basis)
    gram = reorder_rows(reorder_columns(gram, width), width)
    basis = reorder_columns(basis, width)
    return (gram, basis)

def diagonalize(gram):
    basis = jnp.eye(gram.shape[0], dtype=jnp.float32)
    for inner in range(STEPS):
        gram, basis = turn_pair(gram, basis)
    return basis

def reference(matrix, flips):
    blocks = matrix.reshape(ROWS, PAIRS, 2, BLOCK)
    upper = blocks[:, :, 0, :]
    lower_half = blocks[:, :, 1, :]
    for round_index in range(ROUNDS):
        paired = jnp.concatenate([upper, lower_half], axis=-1)
        grams = jnp.einsum('rpi,rpj->pij', paired, paired, precision=HIGH, preferred_element_type=jnp.float32)
        bases = lax.map(diagonalize, grams)
        paired = jnp.einsum('rpi,pij->rpj', paired, bases, precision=HIGH, preferred_element_type=jnp.float32)
        new_top = paired[:, :, :BLOCK]
        new_bottom = paired[:, :, BLOCK:]
        flipped = (flips[round_index] == 1)[None, :, None]
        top_swapped = jnp.where(flipped, new_bottom, new_top)
        bottom_swapped = jnp.where(flipped, new_top, new_bottom)
        upper = jnp.concatenate([top_swapped[:, :1], bottom_swapped[:, :1], top_swapped[:, 1:-1]], axis=1)
        lower_half = jnp.concatenate([bottom_swapped[:, 1:], top_swapped[:, -1:]], axis=1)
    return jnp.stack([upper, lower_half], axis=2).reshape(ROWS, COLS)
```

```python
import jax
import jax.numpy as jnp
from jax import lax
from jax.experimental import pallas as pl
from jax.experimental.pallas import tpu as pltpu
from jax.sharding import PartitionSpec as P

ROUNDS = 4
STEPS = 8
W = 128
CHUNKS = 4
HIGH = lax.Precision.HIGHEST
MESH = pl.DeviceIdType.MESH
F32 = jnp.float32


def nt(a, b):
    return lax.dot_general(a, b, (((1,), (1,)), ((), ())), precision=HIGH, preferred_element_type=F32)


def tn(a, b):
    return lax.dot_general(a, b, (((0,), (0,)), ((), ())), precision=HIGH, preferred_element_type=F32)


def rotate_step(src, dst):
    row = lax.broadcasted_iota(jnp.int32, (W, W), 0)
    col = lax.broadcasted_iota(jnp.int32, (W, W), 1)
    eye = row == col
    lane = lax.broadcasted_iota(jnp.int32, (8, W), 1)

    def diag(k):
        return jnp.sum(jnp.where(eye, src[k, 8 : 8 + W], 0.0), axis=0, keepdims=True)

    a, g, b = diag(0), diag(1), diag(3)
    differ = b - a
    sign = jnp.where(differ >= 0, 1.0, -1.0)
    tangent = 2.0 * g * sign / (jnp.abs(differ) + jnp.sqrt(differ * differ + 4.0 * g * g) + 1e-06 * (a + b))
    cos = 1.0 / jnp.sqrt(1.0 + tangent * tangent)
    sin = cos * tangent
    cos_t = jnp.broadcast_to(cos, (W, W)).T
    sin_t = jnp.broadcast_to(sin, (W, W)).T
    c8 = jnp.broadcast_to(cos, (8, W))
    s8 = jnp.broadcast_to(sin, (8, W))

    def reorder(left, right):
        mixed = pltpu.roll(jnp.where(lane == 0, right, left), 1, 1)
        new_left = jnp.where(lane == 0, left, mixed)
        new_right = jnp.where(lane == W - 1, left, pltpu.roll(right, W - 1, 1))
        return new_left, new_right

    def put(k, i, top, bottom):
        lo = 8 * i
        dst[k, 9 + lo : 17 + lo] = top
        dst[k + 2, 7 + lo : 15 + lo] = bottom

    def ends(k, t0, b0, t127):
        dst[k, 8:9] = t0
        dst[k, 9:10] = b0
        dst[k + 2, 7 + W : 8 + W] = t127

    first = None
    for i in range(W // 8):
        at = slice(8 + 8 * i, 16 + 8 * i)
        ct, st = cos_t[8 * i : 8 * i + 8], sin_t[8 * i : 8 * i + 8]
        A, B, C, D = src[0, at], src[1, at], src[2, at], src[3, at]
        A1, B1 = A * c8 - B * s8, A * s8 + B * c8
        C1, D1 = C * c8 - D * s8, C * s8 + D * c8
        A2, C2 = ct * A1 - st * C1, st * A1 + ct * C1
        B2, D2 = ct * B1 - st * D1, st * B1 + ct * D1
        A3, B3 = reorder(A2, B2)
        C3, D3 = reorder(C2, D2)
        put(0, i, A3, C3)
        put(1, i, B3, D3)
        wtl, wtr, wbl, wbr = src[4, at], src[5, at], src[6, at], src[7, at]
        ntl, nbl = ct * wtl - st * wbl, st * wtl + ct * wbl
        ntr, nbr = ct * wtr - st * wbr, st * wtr + ct * wbr
        put(4, i, ntl, nbl)
        put(5, i, ntr, nbr)
        if i == 0:
            first = [(v[0:1], u[0:1]) for v, u in ((A3, C3), (B3, D3), (ntl, nbl), (ntr, nbr))]
    last = [v[7:8] for v in (A3, B3, ntl, ntr)]
    for k, (t0, b0), t127 in zip((0, 1, 4, 5), first, last):
        ends(k, t0, b0, t127)


def kernel(m_ref, flips_ref, out_top, out_bot, top, bot, xs, ys, state, part0, rs0, red0, sum0,
           part, rs, red, cross, gx, gy, gd, in_sem, mx_s, mt_r, my_s, mb_r, gx_s, gt_r, gy_s, gb_r,
           ag_s, ag_r, rs_s, rs_r, bc_s, bc_r):
    p = lax.axis_index("col")
    q = lax.axis_index("row")
    last = lax.axis_size("col") - 1
    n = lax.axis_size("row")
    rows = m_ref.shape[0]
    step = rows // CHUNKS

    loads = []
    for c in range(CHUNKS):
        at = pl.ds(c * step, step)
        for h, buf in enumerate((top, bot)):
            load = pltpu.make_async_copy(m_ref.at[at, pl.ds(h * W, W)], buf.at[0, at], in_sem.at[c, h])
            load.start()
            loads.append(load)

    barrier = pltpu.get_barrier_semaphore()
    for d in range(1, n):
        pl.semaphore_signal(barrier, inc=1, device_id={"row": lax.rem(q + d, n)}, device_id_type=MESH)

    @pl.when(p < last)
    def _():
        pl.semaphore_signal(barrier, inc=1, device_id={"col": p + 1}, device_id_type=MESH)

    @pl.when(p > 0)
    def _():
        pl.semaphore_signal(barrier, inc=1, device_id={"col": p - 1}, device_id_type=MESH)

    def remote(src, dst, s, r, where):
        return pltpu.make_async_remote_copy(
            src_ref=src, dst_ref=dst, send_sem=s, recv_sem=r, device_id=where, device_id_type=MESH)

    def all_reduce(r, size, part, rs, red, out):
        for d in range(1, n):
            t = lax.rem(q + d, n)
            remote(part.at[pl.ds(t * size, size)], rs.at[q], rs_s.at[r, d], rs_r.at[r, d], {"row": t}).start()
        rs[q] = part[pl.ds(pl.multiple_of(q * size, 16), size), :]
        for d in range(1, n):
            t = lax.rem(q + d, n)
            remote(part.at[pl.ds(t * size, size)], rs.at[q], rs_s.at[r, d], rs_r.at[r, d], {"row": t}).wait_recv()
        total = rs[0]
        for j in range(1, n):
            total = total + rs[j]
        red[...] = total
        mine = pl.ds(pl.multiple_of(q * size, 16), size)
        for d in range(1, n):
            t = lax.rem(q + d, n)
            remote(red, out.at[mine], bc_s.at[r, d], bc_r.at[r, d], {"row": t}).start()
        out[mine, :] = total
        for d in range(1, n):
            t = lax.rem(q + d, n)
            remote(red, out.at[mine], bc_s.at[r, d], bc_r.at[r, d], {"row": t}).wait()
            remote(part.at[pl.ds(t * size, size)], rs.at[q], rs_s.at[r, d], rs_r.at[r, d], {"row": t}).wait_send()

    g_tt = g_tb = g_bb = None
    for c in range(CHUNKS):
        loads[2 * c].wait()
        loads[2 * c + 1].wait()
        t = top[0, c * step : (c + 1) * step]
        b = bot[0, c * step : (c + 1) * step]
        tt, tb, bb = tn(t, t), tn(t, b), tn(b, b)
        g_tt = tt if c == 0 else g_tt + tt
        g_tb = tb if c == 0 else g_tb + tb
        g_bb = bb if c == 0 else g_bb + bb
    part0[0:W] = g_tt
    part0[W : 2 * W] = g_tb
    part0[2 * W : 3 * W] = g_bb

    met = n - 1 + (p > 0).astype(jnp.int32) + (p < last).astype(jnp.int32)
    pl.semaphore_wait(barrier, met)

    all_reduce(0, 3 * W // n, part0, rs0, red0, sum0)

    row = lax.broadcasted_iota(jnp.int32, (W, W), 0)
    col = lax.broadcasted_iota(jnp.int32, (W, W), 1)
    eye = jnp.where(row == col, 1.0, 0.0)
    zero = jnp.zeros((W, W), F32)

    for r in range(ROUNDS):
        inner = slice(8, 8 + W)
        if r == 0:
            g_tt, g_tb, g_bb = sum0[0:W], sum0[W : 2 * W], sum0[2 * W : 3 * W]
        else:
            g_tt = gd[r - 1, :, 0].reshape(W, W)
            g_bb = gd[r - 1, :, 1].reshape(W, W)
            g_tb = cross[r - 1]
        state[0, 0, inner] = g_tt
        state[0, 1, inner] = g_tb
        state[0, 2, inner] = g_tb.T
        state[0, 3, inner] = g_bb
        state[0, 4, inner] = eye
        state[0, 5, inner] = zero
        state[0, 6, inner] = zero
        state[0, 7, inner] = eye

        def two(_, carry):
            rotate_step(state.at[0], state.at[1])
            rotate_step(state.at[1], state.at[0])
            return carry

        lax.fori_loop(0, STEPS // 2, two, 0)

        flag = jnp.broadcast_to(flips_ref[r : r + 1, :], (W, W))
        swap = jnp.logical_xor(flag == 1, jnp.broadcast_to(p, (W, W)) == 0)

        def pick(k, j):
            u, v = state[0, k, inner], state[0, j, inner]
            return jnp.where(swap, v, u), jnp.where(swap, u, v)

        xl, yl = pick(4, 6)
        xr, yr = pick(5, 7)

        if r < ROUNDS - 1:
            gx[r], gy[r] = pick(0, 3)
            piece = pl.ds(pl.multiple_of(q * (W // n), 16), W // n)

            def send_gx():
                return remote(gx.at[r, piece], gd.at[r, q, 0], gx_s.at[r], gt_r.at[r], {"col": p + 1})

            def send_gy():
                return remote(gy.at[r, piece], gd.at[r, q, 1], gy_s.at[r], gb_r.at[r], {"col": p - 1})

            def keep_gx():
                return pltpu.make_async_copy(gx.at[r, piece], gd.at[r, q, 1], gb_r.at[r])

            def keep_gy():
                return pltpu.make_async_copy(gy.at[r, piece], gd.at[r, q, 0], gt_r.at[r])

            pl.when(p < last)(lambda: send_gx().start())
            pl.when(p == last)(lambda: keep_gx().start())
            pl.when(p > 0)(lambda: send_gy().start())
            pl.when(p == 0)(lambda: keep_gy().start())

        def dests(r, at):
            if r < ROUNDS - 1:
                return top.at[r + 1, at], bot.at[r + 1, at]
            return out_top.at[at], out_bot.at[at]

        def moves(r, c):
            at = pl.ds(c * step, step)
            to_top, to_bot = dests(r, at)
            right = lambda: remote(xs.at[r, at], to_top, mx_s.at[r, c], mt_r.at[r, c], {"col": p + 1})
            left = lambda: remote(ys.at[r, at], to_bot, my_s.at[r, c], mb_r.at[r, c], {"col": p - 1})
            keep_x = lambda: pltpu.make_async_copy(xs.at[r, at], to_bot, mb_r.at[r, c])
            keep_y = lambda: pltpu.make_async_copy(ys.at[r, at], to_top, mt_r.at[r, c])
            return right, left, keep_x, keep_y

        for c in range(CHUNKS):
            at = slice(c * step, (c + 1) * step)
            right, left, keep_x, keep_y = moves(r, c)
            t, b = top[r, at], bot[r, at]
            xs[r, at] = nt(t, xl) + nt(b, xr)
            pl.when(p < last)(lambda: right().start())
            pl.when(p == last)(lambda: keep_x().start())
            ys[r, at] = nt(t, yl) + nt(b, yr)
            pl.when(p > 0)(lambda: left().start())
            pl.when(p == 0)(lambda: keep_y().start())

        def arrived(c):
            right, left, keep_x, keep_y = moves(r, c)
            keep_y().wait()
            keep_x().wait()

        def sent():
            for c in range(CHUNKS):
                right, left, keep_x, keep_y = moves(r, c)
                pl.when(p < last)(lambda: right().wait_send())
                pl.when(p > 0)(lambda: left().wait_send())

        if r < ROUNDS - 1:
            keep_gy().wait()
            keep_gx().wait()

            def hand(d):
                t = lax.rem(q + d, n)
                return remote(gd.at[r, q], gd.at[r, q], ag_s.at[r, d], ag_r.at[r, d], {"row": t})

            for d in range(1, n):
                hand(d).start()

            total = None
            for c in range(CHUNKS):
                arrived(c)
                at = slice(c * step, (c + 1) * step)
                now = tn(top[r + 1, at], bot[r + 1, at])
                total = now if c == 0 else total + now
            part[r] = total
            all_reduce(r + 1, W // n, part.at[r], rs.at[r], red.at[r], cross.at[r])
            for d in range(1, n):
                hand(d).wait()
            pl.when(p < last)(lambda: send_gx().wait_send())
            pl.when(p > 0)(lambda: send_gy().wait_send())
            sent()
        else:
            for c in range(CHUNKS):
                arrived(c)
            sent()


def body(matrix, flips):
    rows = matrix.shape[0]
    n = lax.axis_size("row")
    R = ROUNDS
    dma = pltpu.SemaphoreType.DMA
    half = jax.ShapeDtypeStruct((rows, W), F32)
    top, bottom = pl.pallas_call(
        kernel,
        out_shape=(half, half),
        in_specs=[pl.BlockSpec(memory_space=pl.ANY), pl.BlockSpec(memory_space=pltpu.VMEM)],
        out_specs=(pl.BlockSpec(memory_space=pl.ANY), pl.BlockSpec(memory_space=pl.ANY)),
        scratch_shapes=[
            pltpu.VMEM((R, rows, W), F32),
            pltpu.VMEM((R, rows, W), F32),
            pltpu.VMEM((R, rows, W), F32),
            pltpu.VMEM((R, rows, W), F32),
            pltpu.VMEM((2, 8, W + 16, W), F32),
            pltpu.VMEM((3 * W, W), F32),
            pltpu.VMEM((n, 3 * W // n, W), F32),
            pltpu.VMEM((3 * W // n, W), F32),
            pltpu.VMEM((3 * W, W), F32),
            pltpu.VMEM((R - 1, W, W), F32),
            pltpu.VMEM((R - 1, n, W // n, W), F32),
            pltpu.VMEM((R - 1, W // n, W), F32),
            pltpu.VMEM((R - 1, W, W), F32),
            pltpu.VMEM((R - 1, W, W), F32),
            pltpu.VMEM((R - 1, W, W), F32),
            pltpu.VMEM((R - 1, n, 2, W // n, W), F32),
            dma((CHUNKS, 2)),
            dma((R, CHUNKS)),
            dma((R, CHUNKS)),
            dma((R, CHUNKS)),
            dma((R, CHUNKS)),
            dma((R,)),
            dma((R,)),
            dma((R,)),
            dma((R,)),
            dma((R, n)),
            dma((R, n)),
            dma((R, n)),
            dma((R, n)),
            dma((R, n)),
            dma((R, n)),
        ],
        compiler_params=pltpu.CompilerParams(
            collective_id=0, has_side_effects=True, vmem_limit_bytes=40 * 1024 * 1024),
    )(matrix, flips)
    return jnp.concatenate([top, bottom], axis=1)


def solution(mesh):
    placed = (P("row", "col"), P(None, "col"))
    return jax.shard_map(
        body, mesh=mesh, in_specs=placed, out_specs=P("row", "col"), check_vma=False
    )
```

```python
import jax
import jax.numpy as jnp
from jax import lax
from jax.experimental import pallas as pl
from jax.experimental.pallas import tpu as pltpu
from jax.sharding import PartitionSpec as P

ROUNDS = 4
STEPS = 8
W = 128
H = W // 2
PAD = 8
CHUNKS = 4
RAW = 2
MESH = pl.DeviceIdType.MESH
F32 = jnp.float32
BF16 = jnp.bfloat16
INNER = slice(PAD, PAD + W)


def dot(a, b, ca, cb):
    return lax.dot_general(a, b, (((ca,), (cb,)), ((), ())), preferred_element_type=F32)


def split(x):
    high = x.astype(BF16)
    return high, (x - high.astype(F32)).astype(BF16)


def full_gram(m):
    high, low = split(m)
    cross = dot(high, low, 0, 0)
    return dot(high, high, 0, 0) + (cross + cross.T)


def cross_gram(t, b):
    four = dot(jnp.concatenate(split(t), axis=1), jnp.concatenate(split(b), axis=1), 0, 0)
    return four[:W, :W] + (four[:W, W:] + four[W:, :W] + four[W:, W:])


def times(t, b, turn):
    high, low = split(jnp.concatenate([t, b], axis=1))
    return dot(high, turn[0], 1, 1) + (dot(high, turn[1], 1, 1) + dot(low, turn[0], 1, 1))


def cos_sin(tangent):
    cos = lax.rsqrt(1.0 + tangent * tangent)
    return cos, cos * tangent


def down(v):
    return jnp.broadcast_to(v, (W, W)).T


def put(dst, k, i, top, bottom):
    lo = PAD + 8 * i
    dst[k, lo + 1 : lo + 9] = top
    dst[k + 2, lo - 1 : lo + 7] = bottom


def put_ends(dst, k, first_top, first_bottom, last_top):
    dst[k, PAD : PAD + 1] = first_top[0:1]
    dst[k, PAD + 1 : PAD + 2] = first_bottom[0:1]
    dst[k + 2, PAD + W - 1 : PAD + W] = last_top[7:8]


def gram_step(src, dst):
    row = lax.broadcasted_iota(jnp.int32, (W, W), 0)
    col = lax.broadcasted_iota(jnp.int32, (W, W), 1)
    eye = row == col
    lane = lax.broadcasted_iota(jnp.int32, (8, W), 1)

    def diag(k):
        return jnp.sum(jnp.where(eye, src[k, INNER], 0.0), axis=0, keepdims=True)

    a, g, b = diag(0), diag(1), diag(3)
    differ = b - a
    sign = jnp.where(differ >= 0, 1.0, -1.0)
    tangent = 2.0 * g * sign / (jnp.abs(differ) + jnp.sqrt(differ * differ + 4.0 * g * g) + 1e-06 * (a + b))
    cos, sin = cos_sin(tangent)
    cos_t, sin_t = down(cos), down(sin)
    c8 = jnp.broadcast_to(cos, (8, W))
    s8 = jnp.broadcast_to(sin, (8, W))

    def reorder(left, right):
        mixed = pltpu.roll(jnp.where(lane == 0, right, left), 1, 1)
        new_left = jnp.where(lane == 0, left, mixed)
        new_right = jnp.where(lane == W - 1, left, pltpu.roll(right, W - 1, 1))
        return new_left, new_right

    first = None
    for i in range(W // 8):
        at = slice(PAD + 8 * i, PAD + 8 * i + 8)
        ct, st = cos_t[8 * i : 8 * i + 8], sin_t[8 * i : 8 * i + 8]
        A, B, C, D = src[0, at], src[1, at], src[2, at], src[3, at]
        A1, B1 = A * c8 - B * s8, A * s8 + B * c8
        C1, D1 = C * c8 - D * s8, C * s8 + D * c8
        A2, C2 = ct * A1 - st * C1, st * A1 + ct * C1
        B2, D2 = ct * B1 - st * D1, st * B1 + ct * D1
        A3, B3 = reorder(A2, B2)
        C3, D3 = reorder(C2, D2)
        put(dst, 0, i, A3, C3)
        put(dst, 1, i, B3, D3)
        if i == 0:
            first = (A3, C3, B3, D3)
    put_ends(dst, 0, first[0], first[1], A3)
    put_ends(dst, 1, first[2], first[3], B3)
    return tangent


def basis_step(src, dst, tangent):
    cos, sin = cos_sin(tangent)
    cos_t, sin_t = down(cos), down(sin)
    first = None
    for i in range(W // 8):
        at = slice(PAD + 8 * i, PAD + 8 * i + 8)
        ct, st = cos_t[8 * i : 8 * i + 8], sin_t[8 * i : 8 * i + 8]
        tl, tr, bl, br = src[0, at], src[1, at], src[2, at], src[3, at]
        ntl, nbl = ct * tl - st * bl, st * tl + ct * bl
        ntr, nbr = ct * tr - st * br, st * tr + ct * br
        put(dst, 0, i, ntl, nbl)
        put(dst, 1, i, ntr, nbr)
        if i == 0:
            first = (ntl, nbl, ntr, nbr)
    put_ends(dst, 0, first[0], first[1], ntl)
    put_ends(dst, 1, first[2], first[3], ntr)


def rebuild(messages, bases):
    row = lax.broadcasted_iota(jnp.int32, (W, W), 0)
    col = lax.broadcasted_iota(jnp.int32, (W, W), 1)
    eye = jnp.where(row == col, 1.0, 0.0)
    zero = jnp.zeros((W, W), F32)
    for base in bases:
        for k, value in enumerate((eye, zero, zero, eye)):
            base[0, k, INNER] = value

    def two(i, carry):
        for half in range(2):
            for message, base in zip(messages, bases):
                basis_step(base.at[half], base.at[1 - half], message[pl.ds(2 * i + half, 1), :])
        return carry

    lax.fori_loop(0, STEPS // 2, two, 0)


def halves(message, base):
    swap = jnp.broadcast_to(message[STEPS : STEPS + 1, :], (W, W)) > 0.5
    tl, tr, bl, br = (base[0, k, INNER] for k in range(4))
    right = jnp.concatenate([jnp.where(swap, bl, tl), jnp.where(swap, br, tr)], axis=1)
    left = jnp.concatenate([jnp.where(swap, tl, bl), jnp.where(swap, tr, br)], axis=1)
    return right, left


def kernel(m_ref, flips_ref, out_top, out_bot, top, bot, xs, ys, ft, fb, lb, rt, gram, base, base_l, base_r,
           part0, sib0, slabs0, sum0, part, sib, slabs, cross, msg, lmsg, rmsg, gx, gy, gt, gb,
           in_sem, ft_s, ft_r, fb_s, fb_r, lb_s, lb_r, rt_s, rt_r, x_s, x_r, y_s, y_r,
           ml_s, ml_r, mr_s, mr_r, gx_s, gt_r, gy_s, gb_r, one_s, one_r, far0_s, far0_r, sib_s, sib_r, far_s, far_r):
    p = lax.axis_index("col")
    q = lax.axis_index("row")
    last = lax.axis_size("col") - 1
    n = lax.axis_size("row")
    rows = m_ref.shape[0]
    step = rows // CHUNKS
    core = lax.rem(q, 2)
    chip = q // 2
    sibling = {"row": q + 1 - 2 * core}
    right = {"col": p + 1}
    left = {"col": p - 1}
    finish = []

    def others(d):
        return {"row": lax.rem(q + 2 * d, n)}

    def part_of(c):
        return pl.ds(c * step, step)

    def remote(src, dst, s, r, where):
        return pltpu.make_async_remote_copy(
            src_ref=src, dst_ref=dst, send_sem=s, recv_sem=r, device_id=where, device_id_type=MESH)

    def go_right(src, dst, s, r):
        pl.when(p < last)(lambda: remote(src, dst, s, r, right).start())
        finish.append(lambda: pl.when(p < last)(lambda: remote(src, dst, s, r, right).wait_send()))

    def go_left(src, dst, s, r):
        pl.when(p > 0)(lambda: remote(src, dst, s, r, left).start())
        finish.append(lambda: pl.when(p > 0)(lambda: remote(src, dst, s, r, left).wait_send()))

    def stay_first(src, dst, r):
        pl.when(p == 0)(lambda: pltpu.make_async_copy(src, dst, r).start())

    def stay_last(src, dst, r):
        pl.when(p == last)(lambda: pltpu.make_async_copy(src, dst, r).start())

    def arrived(dst, r):
        pltpu.make_async_copy(dst, dst, r).wait()

    loads = []
    for c in range(CHUNKS):
        at = part_of(c)
        for h, buf in enumerate((top, bot)):
            load = pltpu.make_async_copy(m_ref.at[at, pl.ds(h * W, W)], buf.at[0, at], in_sem.at[c, h])
            load.start()
            loads.append(load)

    barrier = pltpu.get_barrier_semaphore()
    for where in [sibling] + [others(d) for d in range(1, n // 2)]:
        pl.semaphore_signal(barrier, inc=1, device_id=where, device_id_type=MESH)

    @pl.when(p < last)
    def _():
        pl.semaphore_signal(barrier, inc=1, device_id=right, device_id_type=MESH)

    @pl.when(p > 0)
    def _():
        pl.semaphore_signal(barrier, inc=1, device_id=left, device_id_type=MESH)

    def sum_first():
        near = remote(part0.at[1 - core], sib0, one_s.at[0], one_r.at[0], sibling)
        near.start()
        near.wait_recv()
        slabs0[chip] = part0[core] + sib0[...]
        far = [
            remote(slabs0.at[chip], slabs0.at[chip], far0_s.at[d], far0_r.at[d], others(d))
            for d in range(1, n // 2)
        ]
        for copy in far:
            copy.start()
        for copy in far:
            copy.wait_recv()
        total = slabs0[0]
        for j in range(1, n // 2):
            total = total + slabs0[j]
        sum0[core] = total
        back = remote(sum0.at[core], sum0.at[core], one_s.at[1], one_r.at[1], sibling)
        back.start()
        back.wait_recv()
        for copy in [near, back] + far:
            finish.append(copy.wait_send)

    def sum_small(r):
        near = remote(part.at[r], sib.at[r], sib_s.at[r], sib_r.at[r], sibling)
        near.start()
        near.wait_recv()
        slabs[r, chip] = part[r] + sib[r]
        far = [
            remote(slabs.at[r, chip], slabs.at[r, chip], far_s.at[r, d], far_r.at[r, d], others(d))
            for d in range(1, n // 2)
        ]
        for copy in far:
            copy.start()
        for copy in far:
            copy.wait_recv()
        total = slabs[r, 0]
        for j in range(1, n // 2):
            total = total + slabs[r, j]
        cross[r] = total
        for copy in [near] + far:
            finish.append(copy.wait_send)

    total = None
    for c in range(CHUNKS):
        loads[2 * c].wait()
        loads[2 * c + 1].wait()
        at = slice(c * step, (c + 1) * step)
        now = full_gram(jnp.concatenate([top[0, at], bot[0, at]], axis=1))
        total = now if c == 0 else total + now
    part0[0, 0:W] = total[:W, :W]
    part0[0, W:] = total[:H, W:]
    part0[1, 0:H] = total[H:W, W:]
    part0[1, H:] = total[W:, W:]

    met = n // 2 + (p > 0).astype(jnp.int32) + (p < last).astype(jnp.int32)
    pl.semaphore_wait(barrier, met)

    def forward(r, c):
        at = part_of(c)
        go_right(top.at[r, at], ft.at[r, at], ft_s.at[r, c], ft_r.at[r, c])
        go_left(bot.at[r, at], fb.at[r, at], fb_s.at[r, c], fb_r.at[r, c])
        stay_first(top.at[r, at], ft.at[r, at], ft_r.at[r, c])
        stay_last(bot.at[r, at], fb.at[r, at], fb_r.at[r, c])

    for c in range(RAW):
        at = part_of(c)
        forward(0, c)
        go_right(bot.at[0, at], lb.at[at], lb_s.at[c], lb_r.at[c])
        go_left(top.at[0, at], rt.at[at], rt_s.at[c], rt_r.at[c])
        stay_first(bot.at[0, at], lb.at[at], lb_r.at[c])
        stay_last(top.at[0, at], rt.at[at], rt_r.at[c])

    sum_first()

    for r in range(ROUNDS):
        if r == 0:
            g_tt, g_bb = sum0[0, 0:W], sum0[1, H:]
            g_tb = jnp.concatenate([sum0[0, W:], sum0[1, 0:H]], axis=0)
        else:
            arrived(gt.at[r - 1], gt_r.at[r - 1])
            arrived(gb.at[r - 1], gb_r.at[r - 1])
            g_tt, g_bb, g_tb = gt[r - 1], gb[r - 1], cross[r - 1]
        for k, value in enumerate((g_tt, g_tb, g_tb.T, g_bb)):
            gram[0, k, INNER] = value

        def two(i, carry):
            msg[r, pl.ds(2 * i, 1)] = gram_step(gram.at[0], gram.at[1])
            msg[r, pl.ds(2 * i + 1, 1)] = gram_step(gram.at[1], gram.at[0])
            return carry

        lax.fori_loop(0, STEPS // 2, two, 0)
        flag = jnp.broadcast_to(flips_ref[:, r : r + 1], (8, W)) == 1
        swap = jnp.logical_xor(flag, jnp.broadcast_to(p, (8, W)) == 0)
        msg[r, STEPS:] = jnp.where(swap, 1.0, 0.0)
        go_right(msg.at[r], lmsg.at[r], ml_s.at[r], ml_r.at[r])
        go_left(msg.at[r], rmsg.at[r], mr_s.at[r], mr_r.at[r])
        stay_first(msg.at[r], lmsg.at[r], ml_r.at[r])
        stay_last(msg.at[r], rmsg.at[r], mr_r.at[r])

        if r < ROUNDS - 1:
            swaps = jnp.broadcast_to(msg[r, STEPS : STEPS + 1], (W, W)) > 0.5
            u, v = gram[0, 0, INNER], gram[0, 3, INNER]
            gx[r] = jnp.where(swaps, v, u)
            gy[r] = jnp.where(swaps, u, v)
            go_right(gx.at[r], gt.at[r], gx_s.at[r], gt_r.at[r])
            go_left(gy.at[r], gb.at[r], gy_s.at[r], gb_r.at[r])
            stay_last(gx.at[r], gb.at[r], gb_r.at[r])
            stay_first(gy.at[r], gt.at[r], gt_r.at[r])

        rebuild([msg.at[r]], [base])
        turn = split(jnp.concatenate(halves(msg.at[r], base), axis=0))
        for c in [*range(RAW, CHUNKS), *range(RAW)]:
            at = slice(c * step, (c + 1) * step)
            new = times(top[r, at], bot[r, at], turn)
            xs[r, at] = new[:, :W]
            ys[r, at] = new[:, W:]
            if r == 0 and c >= RAW:
                src = part_of(c)
                go_right(xs.at[r, src], top.at[1, src], x_s.at[c], x_r.at[c])
                go_left(ys.at[r, src], bot.at[1, src], y_s.at[c], y_r.at[c])
                stay_first(ys.at[r, src], top.at[1, src], x_r.at[c])
                stay_last(xs.at[r, src], bot.at[1, src], y_r.at[c])

        arrived(lmsg.at[r], ml_r.at[r])
        arrived(rmsg.at[r], mr_r.at[r])
        rebuild([lmsg.at[r], rmsg.at[r]], [base_l, base_r])
        turn_l = split(halves(lmsg.at[r], base_l)[0])
        turn_r = split(halves(rmsg.at[r], base_r)[1])
        at_first = jnp.broadcast_to(p, (step, W)) == 0
        at_last = jnp.broadcast_to(p, (step, W)) == last
        total = None
        for c in range(CHUNKS):
            at = slice(c * step, (c + 1) * step)
            ref = part_of(c)
            if r == 0 and c >= RAW:
                arrived(top.at[1, ref], x_r.at[c])
                arrived(bot.at[1, ref], y_r.at[c])
                new_top, new_bot = top[1, at], bot[1, at]
            else:
                arrived(ft.at[r, ref], ft_r.at[r, c])
                arrived(fb.at[r, ref], fb_r.at[r, c])
                if r == 0:
                    arrived(lb.at[ref], lb_r.at[c])
                    arrived(rt.at[ref], rt_r.at[c])
                    l_b, r_t = lb[at], rt[at]
                else:
                    l_b, r_t = ys[r - 1, at], xs[r - 1, at]
                new_top = jnp.where(at_first, ys[r, at], times(ft[r, at], l_b, turn_l))
                new_bot = jnp.where(at_last, xs[r, at], times(r_t, fb[r, at], turn_r))
                if r < ROUNDS - 1:
                    top[r + 1, at] = new_top
                    bot[r + 1, at] = new_bot
                else:
                    out_top[at] = new_top
                    out_bot[at] = new_bot
            if r < ROUNDS - 1:
                forward(r + 1, c)
                now = cross_gram(new_top, new_bot)
                total = now if c == 0 else total + now
        if r < ROUNDS - 1:
            part[r] = total
            sum_small(r)

    for wait in finish:
        wait()


def body(matrix, flips):
    rows = matrix.shape[0]
    n = lax.axis_size("row")
    R = ROUNDS
    C = CHUNKS
    dma = pltpu.SemaphoreType.DMA
    half = jax.ShapeDtypeStruct((rows, W), F32)

    def vmem(*shape):
        return pltpu.VMEM(shape, F32)

    top, bottom = pl.pallas_call(
        kernel,
        out_shape=(half, half),
        in_specs=[pl.BlockSpec(memory_space=pl.ANY), pl.BlockSpec(memory_space=pltpu.VMEM)],
        out_specs=(pl.BlockSpec(memory_space=pltpu.VMEM), pl.BlockSpec(memory_space=pltpu.VMEM)),
        scratch_shapes=[
            *(vmem(R, rows, W) for _ in range(6)),
            *(vmem(rows, W) for _ in range(2)),
            *(vmem(2, 4, W + 2 * PAD, W) for _ in range(4)),
            vmem(2, W + H, W),
            vmem(W + H, W),
            vmem(n // 2, W + H, W),
            vmem(2, W + H, W),
            vmem(R - 1, W, W),
            vmem(R - 1, W, W),
            vmem(R - 1, n // 2, W, W),
            vmem(R - 1, W, W),
            *(vmem(R, 2 * STEPS, W) for _ in range(3)),
            *(vmem(R - 1, W, W) for _ in range(4)),
            dma((C, 2)),
            *(dma((R, C)) for _ in range(4)),
            *(dma((C,)) for _ in range(8)),
            *(dma((R,)) for _ in range(8)),
            dma((2,)),
            dma((2,)),
            dma((n // 2,)),
            dma((n // 2,)),
            dma((R,)),
            dma((R,)),
            dma((R, n // 2)),
            dma((R, n // 2)),
        ],
        compiler_params=pltpu.CompilerParams(
            collective_id=0, has_side_effects=True, vmem_limit_bytes=60 * 1024 * 1024),
    )(matrix, flips.T)
    return jnp.concatenate([top, bottom], axis=1)


def solution(mesh):
    placed = (P("row", "col"), P(None, "col"))
    return jax.shard_map(
        body, mesh=mesh, in_specs=placed, out_specs=P("row", "col"), check_vma=False
    )
```

```python
import jax
import jax.numpy as jnp
from jax import lax
from jax.experimental import pallas as pl
from jax.experimental.pallas import tpu as pltpu
from jax.sharding import PartitionSpec as P

ROUNDS = 4
STEPS = 8
W = 128
H = W // 2
PAD = 8
SIZES = (320, 320, 192, 192)
CHUNKS = len(SIZES)
RAW = 2
PART = STEPS // 2
MESH = pl.DeviceIdType.MESH
F32 = jnp.float32
BF16 = jnp.bfloat16
INNER = slice(PAD, PAD + W)


def dot(a, b, ca, cb):
    return lax.dot_general(a, b, (((ca,), (cb,)), ((), ())), preferred_element_type=F32)


def split(x):
    high = x.astype(BF16)
    return high, (x - high.astype(F32)).astype(BF16)


def full_gram(m):
    high, low = split(m)
    cross = dot(high, low, 0, 0)
    return dot(high, high, 0, 0) + (cross + cross.T)


def cross_gram(t, b):
    four = dot(jnp.concatenate(split(t), axis=1), jnp.concatenate(split(b), axis=1), 0, 0)
    return four[:W, :W] + (four[:W, W:] + four[W:, :W] + four[W:, W:])


def times(t, b, turn):
    high, low = split(jnp.concatenate([t, b], axis=1))
    return dot(high, turn[0], 1, 1) + (dot(high, turn[1], 1, 1) + dot(low, turn[0], 1, 1))


def cos_sin(tangent):
    cos = lax.rsqrt(1.0 + tangent * tangent)
    return cos, cos * tangent


def down(v):
    return jnp.broadcast_to(v, (W, W)).T


def put(dst, k, i, top, bottom):
    lo = PAD + 8 * i
    dst[k, lo + 1 : lo + 9] = top
    dst[k + 2, lo - 1 : lo + 7] = bottom


def put_ends(dst, k, first_top, first_bottom, last_top):
    dst[k, PAD : PAD + 1] = first_top[0:1]
    dst[k, PAD + 1 : PAD + 2] = first_bottom[0:1]
    dst[k + 2, PAD + W - 1 : PAD + W] = last_top[7:8]


def pick_start(src):
    row = lax.broadcasted_iota(jnp.int32, (8, W), 0)
    lane = lax.broadcasted_iota(jnp.int32, (8, W), 1)
    sums = []
    for k in (0, 1, 3):
        total = None
        for i in range(W // 8):
            now = jnp.where(lane == row + 8 * i, src[k, PAD + 8 * i : PAD + 8 * i + 8], 0.0)
            total = now if i == 0 else total + now
        sums.append(jnp.broadcast_to(jnp.sum(total, axis=0, keepdims=True), (8, W)))
    return tuple(sums)


def gram_step(src, dst, picked):
    row = lax.broadcasted_iota(jnp.int32, (8, W), 0)
    lane = lax.broadcasted_iota(jnp.int32, (8, W), 1)
    a, g, b = picked
    differ = b - a
    sign = jnp.where(differ >= 0, 1.0, -1.0)
    tangent = 2.0 * g * sign / (jnp.abs(differ) + jnp.sqrt(differ * differ + 4.0 * g * g) + 1e-06 * (a + b))
    c8, s8 = cos_sin(tangent)
    cos_t, sin_t = down(c8[0:1]), down(s8[0:1])

    def reorder(left, right):
        mixed = pltpu.roll(jnp.where(lane == 0, right, left), 1, 1)
        new_left = jnp.where(lane == 0, left, mixed)
        new_right = jnp.where(lane == W - 1, left, pltpu.roll(right, W - 1, 1))
        return new_left, new_right

    def add(total, mask, value):
        value = jnp.where(mask, value, 0.0)
        return value if total is None else total + value

    first = a_next = g_next = b_next = None
    for i in range(W // 8):
        at = slice(PAD + 8 * i, PAD + 8 * i + 8)
        ct, st = cos_t[8 * i : 8 * i + 8], sin_t[8 * i : 8 * i + 8]
        A, B, C, D = src[0, at], src[1, at], src[2, at], src[3, at]
        A1, B1 = A * c8 - B * s8, A * s8 + B * c8
        C1, D1 = C * c8 - D * s8, C * s8 + D * c8
        A2, C2 = ct * A1 - st * C1, st * A1 + ct * C1
        B2, D2 = ct * B1 - st * D1, st * B1 + ct * D1
        A3, B3 = reorder(A2, B2)
        C3, D3 = reorder(C2, D2)
        put(dst, 0, i, A3, C3)
        put(dst, 1, i, B3, D3)
        up = lane == row + (8 * i + 1)
        if i == 0:
            first = (A3, C3, B3, D3)
            up = jnp.logical_or(jnp.logical_and(up, row > 0), jnp.logical_and(lane == 0, row == 0))
            second = jnp.logical_and(lane == 1, row == 0)
            a_next = add(a_next, second, C3)
            g_next = add(g_next, second, D3)
        a_next = add(a_next, up, A3)
        g_next = add(g_next, up, B3)
        b_next = add(b_next, lane == row + (8 * i - 1), D3)
    b_next = add(b_next, jnp.logical_and(lane == W - 1, row == 7), B3)
    put_ends(dst, 0, first[0], first[1], A3)
    put_ends(dst, 1, first[2], first[3], B3)
    picked = tuple(
        jnp.broadcast_to(jnp.sum(v, axis=0, keepdims=True), (8, W)) for v in (a_next, g_next, b_next))
    return tangent[0:1], picked


def basis_step(src, dst, tangent):
    cos, sin = cos_sin(tangent)
    cos_t, sin_t = down(cos), down(sin)
    first = None
    for i in range(W // 8):
        at = slice(PAD + 8 * i, PAD + 8 * i + 8)
        ct, st = cos_t[8 * i : 8 * i + 8], sin_t[8 * i : 8 * i + 8]
        tl, tr, bl, br = src[0, at], src[1, at], src[2, at], src[3, at]
        ntl, nbl = ct * tl - st * bl, st * tl + ct * bl
        ntr, nbr = ct * tr - st * br, st * tr + ct * br
        put(dst, 0, i, ntl, nbl)
        put(dst, 1, i, ntr, nbr)
        if i == 0:
            first = (ntl, nbl, ntr, nbr)
    put_ends(dst, 0, first[0], first[1], ntl)
    put_ends(dst, 1, first[2], first[3], ntr)


def identity(bases):
    row = lax.broadcasted_iota(jnp.int32, (W, W), 0)
    col = lax.broadcasted_iota(jnp.int32, (W, W), 1)
    eye = jnp.where(row == col, 1.0, 0.0)
    zero = jnp.zeros((W, W), F32)
    for base in bases:
        for k, value in enumerate((eye, zero, zero, eye)):
            base[0, k, INNER] = value


def rebuild(parts, bases):
    for i in range(PART):
        for part, base in zip(parts, bases):
            basis_step(base.at[i % 2], base.at[1 - i % 2], part[i : i + 1, :])


def halves(part, base):
    swap = jnp.broadcast_to(part[PART : PART + 1, :], (W, W)) > 0.5
    tl, tr, bl, br = (base[0, k, INNER] for k in range(4))
    right = jnp.concatenate([jnp.where(swap, bl, tl), jnp.where(swap, br, tr)], axis=1)
    left = jnp.concatenate([jnp.where(swap, tl, bl), jnp.where(swap, tr, br)], axis=1)
    return right, left


def kernel(m_ref, flips_ref, out, done, top, bot, xs, ys, ft, fb, lb, rt, gram, base, base_l, base_r,
           part0, sib0, slabs0, sum0, part, sib, slabs, cross, msg, lmsg, rmsg, gx, gy, gt, gb,
           in_sem, out_sem, ft_s, ft_r, fb_s, fb_r, lb_s, lb_r, rt_s, rt_r, x_s, x_r, y_s, y_r,
           ml_s, ml_r, mr_s, mr_r, gx_s, gt_r, gy_s, gb_r, one_s, one_r, far0_s, far0_r, sib_s, sib_r, far_s, far_r):
    p = lax.axis_index("col")
    q = lax.axis_index("row")
    last = lax.axis_size("col") - 1
    n = lax.axis_size("row")
    rows = m_ref.shape[0]
    sizes = [size * rows // 1024 for size in SIZES]
    begins = [sum(sizes[:c]) for c in range(CHUNKS)]
    core = lax.rem(q, 2)
    chip = q // 2
    sibling = {"row": q + 1 - 2 * core}
    right = {"col": p + 1}
    left = {"col": p - 1}
    finish = []

    def others(d):
        return {"row": lax.rem(q + 2 * d, n)}

    def part_of(c):
        return pl.ds(begins[c], sizes[c])

    def rows_of(c):
        return slice(begins[c], begins[c] + sizes[c])

    def remote(src, dst, s, r, where):
        return pltpu.make_async_remote_copy(
            src_ref=src, dst_ref=dst, send_sem=s, recv_sem=r, device_id=where, device_id_type=MESH)

    def go_right(src, dst, s, r):
        pl.when(p < last)(lambda: remote(src, dst, s, r, right).start())
        finish.append(lambda: pl.when(p < last)(lambda: remote(src, dst, s, r, right).wait_send()))

    def go_left(src, dst, s, r):
        pl.when(p > 0)(lambda: remote(src, dst, s, r, left).start())
        finish.append(lambda: pl.when(p > 0)(lambda: remote(src, dst, s, r, left).wait_send()))

    def stay_first(src, dst, r):
        pl.when(p == 0)(lambda: pltpu.make_async_copy(src, dst, r).start())

    def stay_last(src, dst, r):
        pl.when(p == last)(lambda: pltpu.make_async_copy(src, dst, r).start())

    def arrived(dst, r):
        pltpu.make_async_copy(dst, dst, r).wait()

    loads = []
    for c in range(CHUNKS):
        at = part_of(c)
        for h, buf in enumerate((top, bot)):
            load = pltpu.make_async_copy(m_ref.at[at, pl.ds(h * W, W)], buf.at[0, at], in_sem.at[c, h])
            load.start()
            loads.append(load)

    barrier = pltpu.get_barrier_semaphore()
    for where in [sibling] + [others(d) for d in range(1, n // 2)]:
        pl.semaphore_signal(barrier, inc=1, device_id=where, device_id_type=MESH)

    @pl.when(p < last)
    def _():
        pl.semaphore_signal(barrier, inc=1, device_id=right, device_id_type=MESH)

    @pl.when(p > 0)
    def _():
        pl.semaphore_signal(barrier, inc=1, device_id=left, device_id_type=MESH)

    def sum_first():
        near = remote(part0.at[1 - core], sib0, one_s.at[0], one_r.at[0], sibling)
        near.start()
        near.wait_recv()
        slabs0[chip] = part0[core] + sib0[...]
        far = [
            remote(slabs0.at[chip], slabs0.at[chip], far0_s.at[d], far0_r.at[d], others(d))
            for d in range(1, n // 2)
        ]
        for copy in far:
            copy.start()
        for copy in far:
            copy.wait_recv()
        total = slabs0[0]
        for j in range(1, n // 2):
            total = total + slabs0[j]
        sum0[core] = total
        back = remote(sum0.at[core], sum0.at[core], one_s.at[1], one_r.at[1], sibling)
        back.start()
        back.wait_recv()
        for copy in [near, back] + far:
            finish.append(copy.wait_send)

    def sum_small(r, old):
        near = remote(part.at[r], sib.at[r], sib_s.at[r], sib_r.at[r], sibling)
        near.start()
        near.wait_recv()
        slabs[r, chip] = part[r] + sib[r]
        far = [
            remote(slabs.at[r, chip], slabs.at[r, chip], far_s.at[r, d], far_r.at[r, d], others(d))
            for d in range(1, n // 2)
        ]
        for copy in far:
            copy.start()
        for wait in old:
            wait()
        for copy in far:
            copy.wait_recv()
        total = slabs[r, 0]
        for j in range(1, n // 2):
            total = total + slabs[r, j]
        cross[r] = total
        for copy in [near] + far:
            finish.append(copy.wait_send)

    total = None
    for c in range(CHUNKS):
        loads[2 * c].wait()
        loads[2 * c + 1].wait()
        at = rows_of(c)
        now = full_gram(jnp.concatenate([top[0, at], bot[0, at]], axis=1))
        total = now if c == 0 else total + now
    upper, lower = total[:W, :W], total[W:, W:]
    row = lax.broadcasted_iota(jnp.int32, (W, W), 0)
    col = lax.broadcasted_iota(jnp.int32, (W, W), 1)
    both = jnp.where(row <= col, upper, lower)
    ends = jnp.sum(jnp.where(row == col, lower, 0.0), axis=0, keepdims=True)
    for h in range(2):
        part0[h, 0:H] = both[h * H : (h + 1) * H]
        part0[h, H:W] = total[h * H : (h + 1) * H, W:]
        part0[h, W:] = jnp.broadcast_to(ends, (8, W))

    met = n // 2 + (p > 0).astype(jnp.int32) + (p < last).astype(jnp.int32)
    pl.semaphore_wait(barrier, met)

    def forward(r, c):
        at = part_of(c)
        go_right(top.at[r, at], ft.at[r, at], ft_s.at[r, c], ft_r.at[r, c])
        go_left(bot.at[r, at], fb.at[r, at], fb_s.at[r, c], fb_r.at[r, c])
        stay_first(top.at[r, at], ft.at[r, at], ft_r.at[r, c])
        stay_last(bot.at[r, at], fb.at[r, at], fb_r.at[r, c])

    for c in range(RAW):
        at = part_of(c)
        forward(0, c)
        go_right(bot.at[0, at], lb.at[at], lb_s.at[c], lb_r.at[c])
        go_left(top.at[0, at], rt.at[at], rt_s.at[c], rt_r.at[c])
        stay_first(bot.at[0, at], lb.at[at], lb_r.at[c])
        stay_last(top.at[0, at], rt.at[at], rt_r.at[c])

    sum_first()

    for r in range(ROUNDS):
        if r == 0:
            g_tb = jnp.concatenate([sum0[0, H:W], sum0[1, H:W]], axis=0)
            both = jnp.concatenate([sum0[0, 0:H], sum0[1, 0:H]], axis=0)
            both_t = both.T
            ends = jnp.broadcast_to(sum0[0, W : W + 1], (W, W))
            g_tt = jnp.where(row <= col, both, both_t)
            g_bb = jnp.where(row > col, both, jnp.where(row < col, both_t, ends))
        else:
            arrived(gt.at[r - 1], gt_r.at[r - 1])
            arrived(gb.at[r - 1], gb_r.at[r - 1])
            g_tt, g_bb, g_tb = gt[r - 1], gb[r - 1], cross[r - 1]
        for k, value in enumerate((g_tt, g_tb, g_tb.T, g_bb)):
            gram[0, k, INNER] = value

        flag = jnp.broadcast_to(flips_ref[:, r : r + 1], (8, W)) == 1
        swap = jnp.logical_xor(flag, jnp.broadcast_to(p, (8, W)) == 0)
        picked = pick_start(gram.at[0])
        for h in range(2):

            def two(i, carry):
                now, carry = gram_step(gram.at[0], gram.at[1], carry)
                msg[r, h, pl.ds(2 * i, 1)] = now
                now, carry = gram_step(gram.at[1], gram.at[0], carry)
                msg[r, h, pl.ds(2 * i + 1, 1)] = now
                return carry

            picked = lax.fori_loop(0, PART // 2, two, picked)
            msg[r, h, PART:] = jnp.where(swap[:PART], 1.0, 0.0)
            go_right(msg.at[r, h], lmsg.at[r, h], ml_s.at[r, h], ml_r.at[r, h])
            go_left(msg.at[r, h], rmsg.at[r, h], mr_s.at[r, h], mr_r.at[r, h])
            stay_first(msg.at[r, h], lmsg.at[r, h], ml_r.at[r, h])
            stay_last(msg.at[r, h], rmsg.at[r, h], mr_r.at[r, h])
        if r > 0:
            forward(r, CHUNKS - 1)

        if r < ROUNDS - 1:
            swaps = jnp.broadcast_to(msg[r, 0, PART : PART + 1], (W, W)) > 0.5
            u, v = gram[0, 0, INNER], gram[0, 3, INNER]
            gx[r] = jnp.where(swaps, v, u)
            gy[r] = jnp.where(swaps, u, v)
            go_right(gx.at[r], gt.at[r], gx_s.at[r], gt_r.at[r])
            go_left(gy.at[r], gb.at[r], gy_s.at[r], gb_r.at[r])
            stay_last(gx.at[r], gb.at[r], gb_r.at[r])
            stay_first(gy.at[r], gt.at[r], gt_r.at[r])

        identity([base, base_l, base_r])
        for h in range(2):
            rebuild([msg.at[r, h]], [base])
        turn = split(jnp.concatenate(halves(msg.at[r, 0], base), axis=0))
        for c in [*range(RAW, CHUNKS), *range(RAW)]:
            at = rows_of(c)
            new = times(top[r, at], bot[r, at], turn)
            xs[r, at] = new[:, :W]
            ys[r, at] = new[:, W:]
            if r == 0 and c >= RAW:
                src = part_of(c)
                go_right(xs.at[r, src], top.at[1, src], x_s.at[c], x_r.at[c])
                go_left(ys.at[r, src], bot.at[1, src], y_s.at[c], y_r.at[c])
                stay_first(ys.at[r, src], top.at[1, src], x_r.at[c])
                stay_last(xs.at[r, src], bot.at[1, src], y_r.at[c])

        for h in range(2):
            arrived(lmsg.at[r, h], ml_r.at[r, h])
            arrived(rmsg.at[r, h], mr_r.at[r, h])
            rebuild([lmsg.at[r, h], rmsg.at[r, h]], [base_l, base_r])
        turn_l = split(halves(lmsg.at[r, 0], base_l)[0])
        turn_r = split(halves(rmsg.at[r, 0], base_r)[1])
        old = []
        if r < ROUNDS - 1:
            old = list(finish)
            finish.clear()
        total = None
        for c in range(CHUNKS):
            at = rows_of(c)
            ref = part_of(c)
            if r == 0 and c >= RAW:
                arrived(top.at[1, ref], x_r.at[c])
                arrived(bot.at[1, ref], y_r.at[c])
                new_top, new_bot = top[1, at], bot[1, at]
            else:
                arrived(ft.at[r, ref], ft_r.at[r, c])
                arrived(fb.at[r, ref], fb_r.at[r, c])
                if r == 0:
                    arrived(lb.at[ref], lb_r.at[c])
                    arrived(rt.at[ref], rt_r.at[c])
                    l_b, r_t = lb[at], rt[at]
                else:
                    l_b, r_t = ys[r - 1, at], xs[r - 1, at]
                at_first = jnp.broadcast_to(p, (sizes[c], W)) == 0
                at_last = jnp.broadcast_to(p, (sizes[c], W)) == last
                new_top = jnp.where(at_first, ys[r, at], times(ft[r, at], l_b, turn_l))
                new_bot = jnp.where(at_last, xs[r, at], times(r_t, fb[r, at], turn_r))
                if r < ROUNDS - 1:
                    top[r + 1, at] = new_top
                    bot[r + 1, at] = new_bot
                else:
                    for h, new in enumerate((new_top, new_bot)):
                        done[h, at] = new
                        copy = pltpu.make_async_copy(
                            done.at[h, ref], out.at[ref, pl.ds(h * W, W)], out_sem.at[c, h])
                        copy.start()
                        finish.append(copy.wait)
            if r < ROUNDS - 1:
                if c < CHUNKS - 1:
                    forward(r + 1, c)
                now = cross_gram(new_top, new_bot)
                total = now if c == 0 else total + now
        if r < ROUNDS - 1:
            part[r] = total
            sum_small(r, old)

    for wait in finish:
        wait()


def body(matrix, flips):
    rows = matrix.shape[0]
    n = lax.axis_size("row")
    R = ROUNDS
    C = CHUNKS
    dma = pltpu.SemaphoreType.DMA

    def vmem(*shape):
        return pltpu.VMEM(shape, F32)

    return pl.pallas_call(
        kernel,
        out_shape=jax.ShapeDtypeStruct(matrix.shape, F32),
        in_specs=[pl.BlockSpec(memory_space=pl.ANY), pl.BlockSpec(memory_space=pltpu.VMEM)],
        out_specs=pl.BlockSpec(memory_space=pl.ANY),
        scratch_shapes=[
            vmem(2, rows, W),
            *(vmem(R, rows, W) for _ in range(6)),
            *(vmem(rows, W) for _ in range(2)),
            *(vmem(2, 4, W + 2 * PAD, W) for _ in range(4)),
            vmem(2, W + 8, W),
            vmem(W + 8, W),
            vmem(n // 2, W + 8, W),
            vmem(2, W + 8, W),
            vmem(R - 1, W, W),
            vmem(R - 1, W, W),
            vmem(R - 1, n // 2, W, W),
            vmem(R - 1, W, W),
            *(vmem(R, 2, 2 * PART, W) for _ in range(3)),
            *(vmem(R - 1, W, W) for _ in range(4)),
            dma((C, 2)),
            dma((C, 2)),
            *(dma((R, C)) for _ in range(4)),
            *(dma((C,)) for _ in range(8)),
            *(dma((R, 2)) for _ in range(4)),
            *(dma((R,)) for _ in range(4)),
            dma((2,)),
            dma((2,)),
            dma((n // 2,)),
            dma((n // 2,)),
            dma((R,)),
            dma((R,)),
            dma((R, n // 2)),
            dma((R, n // 2)),
        ],
        compiler_params=pltpu.CompilerParams(
            collective_id=0, has_side_effects=True, vmem_limit_bytes=60 * 1024 * 1024),
    )(matrix, flips.T)


def solution(mesh):
    placed = (P("row", "col"), P(None, "col"))
    return jax.shard_map(
        body, mesh=mesh, in_specs=placed, out_specs=P("row", "col"), check_vma=False
    )
```

```python
import jax
import jax.numpy as jnp
from jax import lax
from jax.experimental import pallas as pl
from jax.experimental.pallas import tpu as pltpu
from jax.sharding import PartitionSpec as P

ROUNDS = 4
STEPS = 8
W = 128
H = W // 2
PAD = 8
SIZES = (512, 384, 128)
CHUNKS = len(SIZES)
RAW = 1
HELD = 1
PART = STEPS // 2
MESH = pl.DeviceIdType.MESH
F32 = jnp.float32
BF16 = jnp.bfloat16
INNER = slice(PAD, PAD + W)


def dot(a, b, ca, cb):
    return lax.dot_general(a, b, (((ca,), (cb,)), ((), ())), preferred_element_type=F32)


def split(x):
    high = x.astype(BF16)
    return high, (x - high.astype(F32)).astype(BF16)


def full_gram(m):
    high, low = split(m)
    cross = dot(high, low, 0, 0)
    return dot(high, high, 0, 0) + (cross + cross.T)


def cross_gram(t, b):
    four = dot(jnp.concatenate(split(t), axis=1), jnp.concatenate(split(b), axis=1), 0, 0)
    return four[:W, :W] + (four[:W, W:] + four[W:, :W] + four[W:, W:])


def times(t, b, turn):
    high, low = split(jnp.concatenate([t, b], axis=1))
    wide = turn.shape[0] // 2
    both = dot(high, turn, 1, 1)
    return both[:, :wide] + (both[:, wide:] + dot(low, turn[:wide], 1, 1))


def side_gram(left, right):
    lh, ll = split(left)
    rh, rl = split(right)
    return dot(lh, rh, 0, 0) + (dot(lh, rl, 0, 0) + dot(ll, rh, 0, 0))


def turned_gram(turn_l, mid, turn_r):
    high, low = split(mid)
    first = dot(turn_l, high, 1, 0)
    first = first[:W] + (first[W:] + dot(turn_l[:W], low, 1, 0))
    high, low = split(first)
    second = dot(high, turn_r, 1, 1)
    return second[:, :W] + (second[:, W:] + dot(low, turn_r[:W], 1, 1))


def stacked(x):
    return jnp.concatenate(split(x), axis=0)


def cos_sin(tangent):
    cos = lax.rsqrt(1.0 + tangent * tangent)
    return cos, cos * tangent


def down(v):
    return jnp.broadcast_to(v, (W, W)).T


def put(dst, k, i, top, bottom):
    lo = PAD + 8 * i
    dst[k, lo + 1 : lo + 9] = top
    dst[k + 2, lo - 1 : lo + 7] = bottom


def put_ends(dst, k, first_top, first_bottom, last_top):
    dst[k, PAD : PAD + 1] = first_top[0:1]
    dst[k, PAD + 1 : PAD + 2] = first_bottom[0:1]
    dst[k + 2, PAD + W - 1 : PAD + W] = last_top[7:8]


def pick_start(src):
    row = lax.broadcasted_iota(jnp.int32, (8, W), 0)
    lane = lax.broadcasted_iota(jnp.int32, (8, W), 1)
    sums = []
    for k in (0, 1, 3):
        total = None
        for i in range(W // 8):
            now = jnp.where(lane == row + 8 * i, src[k, PAD + 8 * i : PAD + 8 * i + 8], 0.0)
            total = now if i == 0 else total + now
        sums.append(jnp.broadcast_to(jnp.sum(total, axis=0, keepdims=True), (8, W)))
    return tuple(sums)


def gram_step(src, dst, picked):
    row = lax.broadcasted_iota(jnp.int32, (8, W), 0)
    lane = lax.broadcasted_iota(jnp.int32, (8, W), 1)
    a, g, b = picked
    differ = b - a
    sign = jnp.where(differ >= 0, 1.0, -1.0)
    tangent = 2.0 * g * sign / (jnp.abs(differ) + jnp.sqrt(differ * differ + 4.0 * g * g) + 1e-06 * (a + b))
    c8, s8 = cos_sin(tangent)
    cos_t, sin_t = down(c8[0:1]), down(s8[0:1])

    def reorder(left, right):
        mixed = pltpu.roll(jnp.where(lane == 0, right, left), 1, 1)
        new_left = jnp.where(lane == 0, left, mixed)
        new_right = jnp.where(lane == W - 1, left, pltpu.roll(right, W - 1, 1))
        return new_left, new_right

    def add(total, mask, value):
        value = jnp.where(mask, value, 0.0)
        return value if total is None else total + value

    first = a_next = g_next = b_next = None
    for i in range(W // 8):
        at = slice(PAD + 8 * i, PAD + 8 * i + 8)
        ct, st = cos_t[8 * i : 8 * i + 8], sin_t[8 * i : 8 * i + 8]
        A, B, C, D = src[0, at], src[1, at], src[2, at], src[3, at]
        A1, B1 = A * c8 - B * s8, A * s8 + B * c8
        C1, D1 = C * c8 - D * s8, C * s8 + D * c8
        A2, C2 = ct * A1 - st * C1, st * A1 + ct * C1
        B2, D2 = ct * B1 - st * D1, st * B1 + ct * D1
        A3, B3 = reorder(A2, B2)
        C3, D3 = reorder(C2, D2)
        put(dst, 0, i, A3, C3)
        put(dst, 1, i, B3, D3)
        up = lane == row + (8 * i + 1)
        if i == 0:
            first = (A3, C3, B3, D3)
            up = jnp.logical_or(jnp.logical_and(up, row > 0), jnp.logical_and(lane == 0, row == 0))
            second = jnp.logical_and(lane == 1, row == 0)
            a_next = add(a_next, second, C3)
            g_next = add(g_next, second, D3)
        a_next = add(a_next, up, A3)
        g_next = add(g_next, up, B3)
        b_next = add(b_next, lane == row + (8 * i - 1), D3)
    b_next = add(b_next, jnp.logical_and(lane == W - 1, row == 7), B3)
    put_ends(dst, 0, first[0], first[1], A3)
    put_ends(dst, 1, first[2], first[3], B3)
    picked = tuple(
        jnp.broadcast_to(jnp.sum(v, axis=0, keepdims=True), (8, W)) for v in (a_next, g_next, b_next))
    return tangent[0:1], picked


def basis_step(src, dst, tangent):
    cos, sin = cos_sin(tangent)
    cos_t, sin_t = down(cos), down(sin)
    first = None
    for i in range(W // 8):
        at = slice(PAD + 8 * i, PAD + 8 * i + 8)
        ct, st = cos_t[8 * i : 8 * i + 8], sin_t[8 * i : 8 * i + 8]
        tl, tr, bl, br = src[0, at], src[1, at], src[2, at], src[3, at]
        ntl, nbl = ct * tl - st * bl, st * tl + ct * bl
        ntr, nbr = ct * tr - st * br, st * tr + ct * br
        put(dst, 0, i, ntl, nbl)
        put(dst, 1, i, ntr, nbr)
        if i == 0:
            first = (ntl, nbl, ntr, nbr)
    put_ends(dst, 0, first[0], first[1], ntl)
    put_ends(dst, 1, first[2], first[3], ntr)


def identity(bases):
    row = lax.broadcasted_iota(jnp.int32, (W, W), 0)
    col = lax.broadcasted_iota(jnp.int32, (W, W), 1)
    eye = jnp.where(row == col, 1.0, 0.0)
    zero = jnp.zeros((W, W), F32)
    for base in bases:
        for k, value in enumerate((eye, zero, zero, eye)):
            base[0, k, INNER] = value


def rebuild(parts, bases):
    for i in range(PART):
        for part, base in zip(parts, bases):
            basis_step(base.at[i % 2], base.at[1 - i % 2], part[i : i + 1, :])


def halves(part, base):
    swap = jnp.broadcast_to(part[PART : PART + 1, :], (W, W)) > 0.5
    tl, tr, bl, br = (base[0, k, INNER] for k in range(4))
    right = jnp.concatenate([jnp.where(swap, bl, tl), jnp.where(swap, br, tr)], axis=1)
    left = jnp.concatenate([jnp.where(swap, tl, bl), jnp.where(swap, tr, br)], axis=1)
    return right, left


def kernel(m_ref, flips_ref, out, done, top, bot, xs, ys, ft, fb, lb, rt, gram, base, base_l, base_r, mid,
           part0, sib0, slabs0, sum0, part, sib, slabs, cross, msg, lmsg, rmsg, gx, gy, gt, gb,
           in_sem, out_sem, ft_s, ft_r, fb_s, fb_r, lb_s, lb_r, rt_s, rt_r, x_s, x_r, y_s, y_r,
           ml_s, ml_r, mr_s, mr_r, gx_s, gt_r, gy_s, gb_r, one_s, one_r, far0_s, far0_r, sib_s, sib_r, far_s, far_r,
           sg_s, sg_r):
    p = lax.axis_index("col")
    q = lax.axis_index("row")
    last = lax.axis_size("col") - 1
    n = lax.axis_size("row")
    rows = m_ref.shape[0]
    sizes = [size * rows // 1024 for size in SIZES]
    begins = [sum(sizes[:c]) for c in range(CHUNKS)]
    core = lax.rem(q, 2)
    chip = q // 2
    sibling = {"row": q + 1 - 2 * core}
    right = {"col": p + 1}
    left = {"col": p - 1}
    finish = []
    mine = pl.ds(pl.multiple_of(core * H, H), H)

    def others(d):
        return {"row": lax.rem(q + 2 * d, n)}

    def part_of(c):
        return pl.ds(begins[c], sizes[c])

    def rows_of(c):
        return slice(begins[c], begins[c] + sizes[c])

    def remote(src, dst, s, r, where):
        return pltpu.make_async_remote_copy(
            src_ref=src, dst_ref=dst, send_sem=s, recv_sem=r, device_id=where, device_id_type=MESH)

    def go_right(src, dst, s, r):
        pl.when(p < last)(lambda: remote(src, dst, s, r, right).start())
        finish.append(lambda: pl.when(p < last)(lambda: remote(src, dst, s, r, right).wait_send()))

    def go_left(src, dst, s, r):
        pl.when(p > 0)(lambda: remote(src, dst, s, r, left).start())
        finish.append(lambda: pl.when(p > 0)(lambda: remote(src, dst, s, r, left).wait_send()))

    def stay_first(src, dst, r):
        pl.when(p == 0)(lambda: pltpu.make_async_copy(src, dst, r).start())

    def stay_last(src, dst, r):
        pl.when(p == last)(lambda: pltpu.make_async_copy(src, dst, r).start())

    def arrived(dst, r):
        pltpu.make_async_copy(dst, dst, r).wait()

    loads = []
    for c in range(CHUNKS):
        at = part_of(c)
        for h, buf in enumerate((top, bot)):
            load = pltpu.make_async_copy(m_ref.at[at, pl.ds(h * W, W)], buf.at[0, at], in_sem.at[c, h])
            load.start()
            loads.append(load)

    barrier = pltpu.get_barrier_semaphore()
    for where in [sibling] + [others(d) for d in range(1, n // 2)]:
        pl.semaphore_signal(barrier, inc=1, device_id=where, device_id_type=MESH)

    @pl.when(p < last)
    def _():
        pl.semaphore_signal(barrier, inc=1, device_id=right, device_id_type=MESH)

    @pl.when(p > 0)
    def _():
        pl.semaphore_signal(barrier, inc=1, device_id=left, device_id_type=MESH)

    def sum_first():
        near = remote(part0.at[1 - core], sib0, one_s.at[0], one_r.at[0], sibling)
        near.start()
        near.wait_recv()
        slabs0[chip] = part0[core] + sib0[...]
        far = [
            remote(slabs0.at[chip], slabs0.at[chip], far0_s.at[d], far0_r.at[d], others(d))
            for d in range(1, n // 2)
        ]
        for copy in far:
            copy.start()
        for copy in far:
            copy.wait_recv()
        total = slabs0[0]
        for j in range(1, n // 2):
            total = total + slabs0[j]
        sum0[core] = total
        back = remote(sum0.at[core], sum0.at[core], one_s.at[1], one_r.at[1], sibling)
        back.start()
        back.wait_recv()
        for copy in [near, back] + far:
            finish.append(copy.wait_send)

    def sum_small(r, between, during):
        near = remote(part.at[r], sib.at[r], sib_s.at[r], sib_r.at[r], sibling)
        near.start()
        between()
        near.wait_recv()
        slabs[r, chip] = part[r] + sib[r]
        far = [
            remote(slabs.at[r, chip], slabs.at[r, chip], far_s.at[r, d], far_r.at[r, d], others(d))
            for d in range(1, n // 2)
        ]
        for copy in far:
            copy.start()
        during()
        for copy in far:
            copy.wait_recv()
        total = slabs[r, 0]
        for j in range(1, n // 2):
            total = total + slabs[r, j]
        cross[r] = total
        for copy in [near] + far:
            finish.append(copy.wait_send)

    total = None
    for c in range(CHUNKS):
        loads[2 * c].wait()
        loads[2 * c + 1].wait()
        at = rows_of(c)
        now = full_gram(jnp.concatenate([top[0, at], bot[0, at]], axis=1))
        total = now if c == 0 else total + now
    upper, lower = total[:W, :W], total[W:, W:]
    row = lax.broadcasted_iota(jnp.int32, (W, W), 0)
    col = lax.broadcasted_iota(jnp.int32, (W, W), 1)
    both = jnp.where(row <= col, upper, lower)
    ends = jnp.sum(jnp.where(row == col, lower, 0.0), axis=0, keepdims=True)
    for h in range(2):
        part0[h, 0:H] = both[h * H : (h + 1) * H]
        part0[h, H:W] = total[h * H : (h + 1) * H, W:]
        part0[h, W:] = jnp.broadcast_to(ends, (8, W))

    met = n // 2 + (p > 0).astype(jnp.int32) + (p < last).astype(jnp.int32)
    pl.semaphore_wait(barrier, met)

    def forward(r, c):
        at = part_of(c)
        go_right(top.at[r, at], ft.at[r, at], ft_s.at[r, c], ft_r.at[r, c])
        go_left(bot.at[r, at], fb.at[r, at], fb_s.at[r, c], fb_r.at[r, c])
        stay_first(top.at[r, at], ft.at[r, at], ft_r.at[r, c])
        stay_last(bot.at[r, at], fb.at[r, at], fb_r.at[r, c])

    for c in range(RAW):
        at = part_of(c)
        forward(0, c)
        go_right(bot.at[0, at], lb.at[at], lb_s.at[c], lb_r.at[c])
        go_left(top.at[0, at], rt.at[at], rt_s.at[c], rt_r.at[c])
        stay_first(bot.at[0, at], lb.at[at], lb_r.at[c])
        stay_last(top.at[0, at], rt.at[at], rt_r.at[c])

    sum_first()

    for r in range(ROUNDS):
        if r == 0:
            g_tb = jnp.concatenate([sum0[0, H:W], sum0[1, H:W]], axis=0)
            both = jnp.concatenate([sum0[0, 0:H], sum0[1, 0:H]], axis=0)
            both_t = both.T
            ends = jnp.broadcast_to(sum0[0, W : W + 1], (W, W))
            g_tt = jnp.where(row <= col, both, both_t)
            g_bb = jnp.where(row > col, both, jnp.where(row < col, both_t, ends))
        else:
            for copy in shares:
                copy.wait_recv()
                finish.append(copy.wait_send)
            g_tt, g_bb, g_tb = gt[r - 1], gb[r - 1], cross[r - 1]
        for k, value in enumerate((g_tt, g_tb, g_tb.T, g_bb)):
            gram[0, k, INNER] = value

        flag = jnp.broadcast_to(flips_ref[:, r : r + 1], (8, W)) == 1
        swap = jnp.logical_xor(flag, jnp.broadcast_to(p, (8, W)) == 0)
        picked = pick_start(gram.at[0])
        for h in range(2):

            def two(i, carry):
                now, carry = gram_step(gram.at[0], gram.at[1], carry)
                msg[r, h, pl.ds(2 * i, 1)] = now
                now, carry = gram_step(gram.at[1], gram.at[0], carry)
                msg[r, h, pl.ds(2 * i + 1, 1)] = now
                return carry

            picked = lax.fori_loop(0, PART // 2, two, picked)
            msg[r, h, PART:] = jnp.where(swap[:PART], 1.0, 0.0)
            go_right(msg.at[r, h], lmsg.at[r, h], ml_s.at[r, h], ml_r.at[r, h])
            go_left(msg.at[r, h], rmsg.at[r, h], mr_s.at[r, h], mr_r.at[r, h])
            stay_first(msg.at[r, h], lmsg.at[r, h], ml_r.at[r, h])
            stay_last(msg.at[r, h], rmsg.at[r, h], mr_r.at[r, h])
        if r > 0:
            for c in range(CHUNKS - HELD, CHUNKS):
                forward(r, c)

        if r < ROUNDS - 1:
            swaps = jnp.broadcast_to(msg[r, 0, PART : PART + 1], (W, W)) > 0.5
            u, v = gram[0, 0, INNER], gram[0, 3, INNER]
            gx[r] = jnp.where(swaps, v, u)
            gy[r] = jnp.where(swaps, u, v)
            go_right(gx.at[r, mine], gt.at[r, mine], gx_s.at[r], gt_r.at[r])
            go_left(gy.at[r, mine], gb.at[r, mine], gy_s.at[r], gb_r.at[r])
            stay_last(gx.at[r, mine], gb.at[r, mine], gb_r.at[r])
            stay_first(gy.at[r, mine], gt.at[r, mine], gt_r.at[r])

        final = r == ROUNDS - 1
        identity([base, base_l, base_r])
        if not final:
            for h in range(2):
                rebuild([msg.at[r, h]], [base])
            turn = stacked(jnp.concatenate(halves(msg.at[r, 0], base), axis=0))
            for c in [*range(RAW, CHUNKS), *range(RAW)]:
                at = rows_of(c)
                new = times(top[r, at], bot[r, at], turn)
                xs[r, at] = new[:, :W]
                ys[r, at] = new[:, W:]
                if r == 0 and c >= RAW:
                    src = part_of(c)
                    go_right(xs.at[r, src], top.at[1, src], x_s.at[c], x_r.at[c])
                    go_left(ys.at[r, src], bot.at[1, src], y_s.at[c], y_r.at[c])
                    stay_first(ys.at[r, src], top.at[1, src], x_r.at[c])
                    stay_last(xs.at[r, src], bot.at[1, src], y_r.at[c])

        raw = range(RAW if r == 0 else CHUNKS)
        late = [c for c in raw if r > 0 and c >= CHUNKS - HELD]

        def wait_raw(c):
            ref = part_of(c)
            arrived(ft.at[r, ref], ft_r.at[r, c])
            arrived(fb.at[r, ref], fb_r.at[r, c])
            if r == 0:
                arrived(lb.at[ref], lb_r.at[c])
                arrived(rt.at[ref], rt_r.at[c])

        def sides(c):
            at = rows_of(c)
            if r == 0:
                l_b, r_t = lb[at], rt[at]
            else:
                l_b = jnp.where(jnp.broadcast_to(p, (sizes[c], W)) == 0, bot[r, at], ys[r - 1, at])
                r_t = jnp.where(jnp.broadcast_to(p, (sizes[c], W)) == last, top[r, at], xs[r - 1, at])
            return jnp.concatenate([ft[r, at], l_b], axis=1), jnp.concatenate([r_t, fb[r, at]], axis=1)

        def add_sides(c):
            wait_raw(c)
            now = side_gram(*sides(c))
            mid[...] = now if c == 0 else mid[...] + now

        def make(c):
            at, ref = rows_of(c), part_of(c)
            l_pair, r_pair = sides(c)
            news = times(l_pair[:, :W], l_pair[:, W:], turn_l), times(r_pair[:, :W], r_pair[:, W:], turn_r)
            if not final:
                top[r + 1, at], bot[r + 1, at] = news
                if c < CHUNKS - HELD:
                    forward(r + 1, c)
                return
            for h, new in enumerate(news):
                done[h, at] = new
                copy = pltpu.make_async_copy(done.at[h, ref], out.at[ref, pl.ds(h * W, W)], out_sem.at[c, h])
                copy.start()
                finish.append(copy.wait)

        for c in raw:
            if c not in late:
                if final:
                    wait_raw(c)
                else:
                    add_sides(c)

        for h in range(2):
            arrived(lmsg.at[r, h], ml_r.at[r, h])
            arrived(rmsg.at[r, h], mr_r.at[r, h])
            rebuild([lmsg.at[r, h], rmsg.at[r, h]], [base_l, base_r])
        goes, stays = halves(lmsg.at[r, 0], base_l)
        turn_l = stacked(jnp.where(jnp.broadcast_to(p, goes.shape) == 0, stays, goes))
        stays, goes = halves(rmsg.at[r, 0], base_r)
        turn_r = stacked(jnp.where(jnp.broadcast_to(p, goes.shape) == last, stays, goes))

        if final:
            for c in raw:
                if c in late:
                    wait_raw(c)
                make(c)
            continue

        old = list(finish)
        finish.clear()
        make(0)
        for c in late:
            add_sides(c)
        total = turned_gram(turn_l, mid[...], turn_r)
        if r == 0:
            for c in range(RAW, CHUNKS):
                at, ref = rows_of(c), part_of(c)
                arrived(top.at[1, ref], x_r.at[c])
                arrived(bot.at[1, ref], y_r.at[c])
                total = total + cross_gram(top[1, at], bot[1, at])
        part[r] = total

        def between():
            if r == 0:
                for c in range(RAW, CHUNKS - HELD):
                    forward(1, c)
            else:
                make(1)

        shares = [
            remote(buf.at[r, mine], buf.at[r, mine], sg_s.at[r, k], sg_r.at[r, k], sibling)
            for k, buf in enumerate((gt, gb))
        ]

        def during():
            arrived(gt.at[r, mine], gt_r.at[r])
            arrived(gb.at[r, mine], gb_r.at[r])
            for copy in shares:
                copy.start()
            if r > 0:
                for c in range(2, CHUNKS):
                    make(c)
            for wait in old:
                wait()

        sum_small(r, between, during)

    for wait in finish:
        wait()


def body(matrix, flips):
    rows = matrix.shape[0]
    n = lax.axis_size("row")
    R = ROUNDS
    C = CHUNKS
    dma = pltpu.SemaphoreType.DMA

    def vmem(*shape):
        return pltpu.VMEM(shape, F32)

    return pl.pallas_call(
        kernel,
        out_shape=jax.ShapeDtypeStruct(matrix.shape, F32),
        in_specs=[pl.BlockSpec(memory_space=pl.ANY), pl.BlockSpec(memory_space=pltpu.VMEM)],
        out_specs=pl.BlockSpec(memory_space=pl.ANY),
        scratch_shapes=[
            vmem(2, rows, W),
            *(vmem(R, rows, W) for _ in range(6)),
            *(vmem(rows, W) for _ in range(2)),
            *(vmem(2, 4, W + 2 * PAD, W) for _ in range(4)),
            vmem(2 * W, 2 * W),
            vmem(2, W + 8, W),
            vmem(W + 8, W),
            vmem(n // 2, W + 8, W),
            vmem(2, W + 8, W),
            vmem(R - 1, W, W),
            vmem(R - 1, W, W),
            vmem(R - 1, n // 2, W, W),
            vmem(R - 1, W, W),
            *(vmem(R, 2, 2 * PART, W) for _ in range(3)),
            *(vmem(R - 1, W, W) for _ in range(4)),
            dma((C, 2)),
            dma((C, 2)),
            *(dma((R, C)) for _ in range(4)),
            *(dma((C,)) for _ in range(8)),
            *(dma((R, 2)) for _ in range(4)),
            *(dma((R,)) for _ in range(4)),
            dma((2,)),
            dma((2,)),
            dma((n // 2,)),
            dma((n // 2,)),
            dma((R,)),
            dma((R,)),
            dma((R, n // 2)),
            dma((R, n // 2)),
            dma((R, 2)),
            dma((R, 2)),
        ],
        compiler_params=pltpu.CompilerParams(
            collective_id=0, has_side_effects=True, vmem_limit_bytes=60 * 1024 * 1024),
    )(matrix, flips.T)


def solution(mesh):
    placed = (P("row", "col"), P(None, "col"))
    return jax.shard_map(
        body, mesh=mesh, in_specs=placed, out_specs=P("row", "col"), check_vma=False
    )
```

```python
import jax
import jax.numpy as jnp
from jax import lax
from jax.experimental import pallas as pl
from jax.experimental.pallas import tpu as pltpu
from jax.sharding import PartitionSpec as P

ROUNDS = 4
STEPS = 8
W = 128
H = W // 2
PAD = 8
SIZES = (448, 448, 128)
CHUNKS = len(SIZES)
RAW = 1
HELD = 1
PART = STEPS // 2
MESH = pl.DeviceIdType.MESH
F32 = jnp.float32
BF16 = jnp.bfloat16
INNER = slice(PAD, PAD + W)


def dot(a, b, ca, cb):
    return lax.dot_general(a, b, (((ca,), (cb,)), ((), ())), preferred_element_type=F32)


def split(x):
    high = x.astype(BF16)
    return high, (x - high.astype(F32)).astype(BF16)


def full_gram(m):
    high, low = split(m)
    cross = dot(high, low, 0, 0)
    return dot(high, high, 0, 0) + (cross + cross.T)


def cross_gram(t, b):
    four = dot(jnp.concatenate(split(t), axis=1), jnp.concatenate(split(b), axis=1), 0, 0)
    return four[:W, :W] + (four[:W, W:] + four[W:, :W] + four[W:, W:])


def times(t, b, turn):
    high, low = split(jnp.concatenate([t, b], axis=1))
    wide = turn.shape[0] // 2
    both = dot(high, turn, 1, 1)
    return both[:, :wide] + (both[:, wide:] + dot(low, turn[:wide], 1, 1))


def side_gram(left, right):
    lh, ll = split(left)
    rh, rl = split(right)
    return dot(lh, rh, 0, 0) + (dot(lh, rl, 0, 0) + dot(ll, rh, 0, 0))


def turned_gram(turn_l, mid, turn_r):
    high, low = split(mid)
    first = dot(turn_l, high, 1, 0)
    first = first[:W] + (first[W:] + dot(turn_l[:W], low, 1, 0))
    high, low = split(first)
    second = dot(high, turn_r, 1, 1)
    return second[:, :W] + (second[:, W:] + dot(low, turn_r[:W], 1, 1))


def stacked(x):
    return jnp.concatenate(split(x), axis=0)


def cos_sin(tangent):
    cos = lax.rsqrt(1.0 + tangent * tangent)
    return cos, cos * tangent


def down(v):
    return jnp.broadcast_to(v, (W, W)).T


def put(dst, k, i, top, bottom):
    lo = PAD + 8 * i
    dst[k, lo + 1 : lo + 9] = top
    dst[k + 2, lo - 1 : lo + 7] = bottom


def put_ends(dst, k, first_top, first_bottom, last_top):
    dst[k, PAD : PAD + 1] = first_top[0:1]
    dst[k, PAD + 1 : PAD + 2] = first_bottom[0:1]
    dst[k + 2, PAD + W - 1 : PAD + W] = last_top[7:8]


def pick_start(src):
    row = lax.broadcasted_iota(jnp.int32, (8, W), 0)
    lane = lax.broadcasted_iota(jnp.int32, (8, W), 1)
    sums = []
    for k in (0, 1, 3):
        total = None
        for i in range(W // 8):
            now = jnp.where(lane == row + 8 * i, src[k, PAD + 8 * i : PAD + 8 * i + 8], 0.0)
            total = now if i == 0 else total + now
        sums.append(jnp.broadcast_to(jnp.sum(total, axis=0, keepdims=True), (8, W)))
    return tuple(sums)


def gram_step(src, dst, picked):
    row = lax.broadcasted_iota(jnp.int32, (8, W), 0)
    lane = lax.broadcasted_iota(jnp.int32, (8, W), 1)
    a, g, b = picked
    differ = b - a
    sign = jnp.where(differ >= 0, 1.0, -1.0)
    tangent = 2.0 * g * sign / (jnp.abs(differ) + jnp.sqrt(differ * differ + 4.0 * g * g) + 1e-06 * (a + b))
    c8, s8 = cos_sin(tangent)
    cos_t, sin_t = down(c8[0:1]), down(s8[0:1])

    def reorder(left, right):
        mixed = pltpu.roll(jnp.where(lane == 0, right, left), 1, 1)
        new_left = jnp.where(lane == 0, left, mixed)
        new_right = jnp.where(lane == W - 1, left, pltpu.roll(right, W - 1, 1))
        return new_left, new_right

    def add(total, mask, value):
        value = jnp.where(mask, value, 0.0)
        return value if total is None else total + value

    first = a_next = g_next = b_next = None
    for i in range(W // 8):
        at = slice(PAD + 8 * i, PAD + 8 * i + 8)
        ct, st = cos_t[8 * i : 8 * i + 8], sin_t[8 * i : 8 * i + 8]
        A, B, C, D = src[0, at], src[1, at], src[2, at], src[3, at]
        A1, B1 = A * c8 - B * s8, A * s8 + B * c8
        C1, D1 = C * c8 - D * s8, C * s8 + D * c8
        A2, C2 = ct * A1 - st * C1, st * A1 + ct * C1
        B2, D2 = ct * B1 - st * D1, st * B1 + ct * D1
        A3, B3 = reorder(A2, B2)
        C3, D3 = reorder(C2, D2)
        put(dst, 0, i, A3, C3)
        put(dst, 1, i, B3, D3)
        up = lane == row + (8 * i + 1)
        if i == 0:
            first = (A3, C3, B3, D3)
            up = jnp.logical_or(jnp.logical_and(up, row > 0), jnp.logical_and(lane == 0, row == 0))
            second = jnp.logical_and(lane == 1, row == 0)
            a_next = add(a_next, second, C3)
            g_next = add(g_next, second, D3)
        a_next = add(a_next, up, A3)
        g_next = add(g_next, up, B3)
        b_next = add(b_next, lane == row + (8 * i - 1), D3)
    b_next = add(b_next, jnp.logical_and(lane == W - 1, row == 7), B3)
    put_ends(dst, 0, first[0], first[1], A3)
    put_ends(dst, 1, first[2], first[3], B3)
    picked = tuple(
        jnp.broadcast_to(jnp.sum(v, axis=0, keepdims=True), (8, W)) for v in (a_next, g_next, b_next))
    return tangent[0:1], picked


def basis_step(src, dst, tangent):
    cos, sin = cos_sin(tangent)
    cos_t, sin_t = down(cos), down(sin)
    first = None
    for i in range(W // 8):
        at = slice(PAD + 8 * i, PAD + 8 * i + 8)
        ct, st = cos_t[8 * i : 8 * i + 8], sin_t[8 * i : 8 * i + 8]
        tl, tr, bl, br = src[0, at], src[1, at], src[2, at], src[3, at]
        ntl, nbl = ct * tl - st * bl, st * tl + ct * bl
        ntr, nbr = ct * tr - st * br, st * tr + ct * br
        put(dst, 0, i, ntl, nbl)
        put(dst, 1, i, ntr, nbr)
        if i == 0:
            first = (ntl, nbl, ntr, nbr)
    put_ends(dst, 0, first[0], first[1], ntl)
    put_ends(dst, 1, first[2], first[3], ntr)


def identity(bases):
    row = lax.broadcasted_iota(jnp.int32, (W, W), 0)
    col = lax.broadcasted_iota(jnp.int32, (W, W), 1)
    eye = jnp.where(row == col, 1.0, 0.0)
    zero = jnp.zeros((W, W), F32)
    for base in bases:
        for k, value in enumerate((eye, zero, zero, eye)):
            base[0, k, INNER] = value


def rebuild(parts, bases):
    for i in range(PART):
        for part, base in zip(parts, bases):
            basis_step(base.at[i % 2], base.at[1 - i % 2], part[i : i + 1, :])


def halves(part, base):
    swap = jnp.broadcast_to(part[PART : PART + 1, :], (W, W)) > 0.5
    tl, tr, bl, br = (base[0, k, INNER] for k in range(4))
    right = jnp.concatenate([jnp.where(swap, bl, tl), jnp.where(swap, br, tr)], axis=1)
    left = jnp.concatenate([jnp.where(swap, tl, bl), jnp.where(swap, tr, br)], axis=1)
    return right, left


def kernel(m_ref, flips_ref, out, done, top, bot, xs, ys, ft, fb, lb, rt, gram, base, base_l, base_r, mid,
           part0, sib0, slabs0, sum0, part, sib, slabs, cross, msg, lmsg, rmsg, gx, gy, gt, gb,
           in_sem, out_sem, ft_s, ft_r, fb_s, fb_r, lb_s, lb_r, rt_s, rt_r, x_s, x_r, y_s, y_r,
           ml_s, ml_r, mr_s, mr_r, gx_s, gt_r, gy_s, gb_r, one_s, one_r, far0_s, far0_r, sib_s, sib_r, far_s, far_r,
           sg_s, sg_r):
    p = lax.axis_index("col")
    q = lax.axis_index("row")
    last = lax.axis_size("col") - 1
    n = lax.axis_size("row")
    rows = m_ref.shape[0]
    sizes = [size * rows // 1024 for size in SIZES]
    begins = [sum(sizes[:c]) for c in range(CHUNKS)]
    core = lax.rem(q, 2)
    chip = q // 2
    sibling = {"row": q + 1 - 2 * core}
    right = {"col": p + 1}
    left = {"col": p - 1}
    finish = []
    far_order = sorted(range(1, n // 2), key=lambda d: -min(d, n // 2 - d))
    mine = pl.ds(pl.multiple_of(core * H, H), H)

    def others(d):
        return {"row": lax.rem(q + 2 * d, n)}

    def part_of(c):
        return pl.ds(begins[c], sizes[c])

    def rows_of(c):
        return slice(begins[c], begins[c] + sizes[c])

    def remote(src, dst, s, r, where):
        return pltpu.make_async_remote_copy(
            src_ref=src, dst_ref=dst, send_sem=s, recv_sem=r, device_id=where, device_id_type=MESH)

    def go_right(src, dst, s, r):
        pl.when(p < last)(lambda: remote(src, dst, s, r, right).start())
        finish.append(lambda: pl.when(p < last)(lambda: remote(src, dst, s, r, right).wait_send()))

    def go_left(src, dst, s, r):
        pl.when(p > 0)(lambda: remote(src, dst, s, r, left).start())
        finish.append(lambda: pl.when(p > 0)(lambda: remote(src, dst, s, r, left).wait_send()))

    def stay_first(src, dst, r):
        pl.when(p == 0)(lambda: pltpu.make_async_copy(src, dst, r).start())

    def stay_last(src, dst, r):
        pl.when(p == last)(lambda: pltpu.make_async_copy(src, dst, r).start())

    def arrived(dst, r):
        pltpu.make_async_copy(dst, dst, r).wait()

    loads = []
    for c in range(CHUNKS):
        at = part_of(c)
        for h, buf in enumerate((top, bot)):
            load = pltpu.make_async_copy(m_ref.at[at, pl.ds(h * W, W)], buf.at[0, at], in_sem.at[c, h])
            load.start()
            loads.append(load)

    barrier = pltpu.get_barrier_semaphore()
    for where in [sibling] + [others(d) for d in range(1, n // 2)]:
        pl.semaphore_signal(barrier, inc=1, device_id=where, device_id_type=MESH)

    @pl.when(p < last)
    def _():
        pl.semaphore_signal(barrier, inc=1, device_id=right, device_id_type=MESH)

    @pl.when(p > 0)
    def _():
        pl.semaphore_signal(barrier, inc=1, device_id=left, device_id_type=MESH)

    def sum_first():
        near = remote(part0.at[1 - core], sib0, one_s.at[0], one_r.at[0], sibling)
        near.start()
        near.wait_recv()
        slabs0[chip] = part0[core] + sib0[...]
        far = [
            remote(slabs0.at[chip], slabs0.at[chip], far0_s.at[d], far0_r.at[d], others(d))
            for d in far_order
        ]
        for copy in far:
            copy.start()
        for copy in far:
            copy.wait_recv()
        total = slabs0[0]
        for j in range(1, n // 2):
            total = total + slabs0[j]
        sum0[core] = total
        back = remote(sum0.at[core], sum0.at[core], one_s.at[1], one_r.at[1], sibling)
        back.start()
        back.wait_recv()
        for copy in [near, back] + far:
            finish.append(copy.wait_send)

    def sum_small(r, between, during):
        near = remote(part.at[r], sib.at[r], sib_s.at[r], sib_r.at[r], sibling)
        near.start()
        between()
        near.wait_recv()
        slabs[r, chip] = part[r] + sib[r]
        far = [
            remote(slabs.at[r, chip], slabs.at[r, chip], far_s.at[r, d], far_r.at[r, d], others(d))
            for d in far_order
        ]
        for copy in far:
            copy.start()
        during()
        for copy in far:
            copy.wait_recv()
        total = slabs[r, 0]
        for j in range(1, n // 2):
            total = total + slabs[r, j]
        cross[r] = total
        for copy in [near] + far:
            finish.append(copy.wait_send)

    total = None
    for c in range(CHUNKS):
        loads[2 * c].wait()
        loads[2 * c + 1].wait()
        at = rows_of(c)
        now = full_gram(jnp.concatenate([top[0, at], bot[0, at]], axis=1))
        total = now if c == 0 else total + now
    upper, lower = total[:W, :W], total[W:, W:]
    row = lax.broadcasted_iota(jnp.int32, (W, W), 0)
    col = lax.broadcasted_iota(jnp.int32, (W, W), 1)
    both = jnp.where(row <= col, upper, lower)
    ends = jnp.sum(jnp.where(row == col, lower, 0.0), axis=0, keepdims=True)
    for h in range(2):
        part0[h, 0:H] = both[h * H : (h + 1) * H]
        part0[h, H:W] = total[h * H : (h + 1) * H, W:]
        part0[h, W:] = jnp.broadcast_to(ends, (8, W))

    met = n // 2 + (p > 0).astype(jnp.int32) + (p < last).astype(jnp.int32)
    pl.semaphore_wait(barrier, met)

    def forward(r, c):
        at = part_of(c)
        go_right(top.at[r, at], ft.at[r, at], ft_s.at[r, c], ft_r.at[r, c])
        go_left(bot.at[r, at], fb.at[r, at], fb_s.at[r, c], fb_r.at[r, c])
        stay_first(top.at[r, at], ft.at[r, at], ft_r.at[r, c])
        stay_last(bot.at[r, at], fb.at[r, at], fb_r.at[r, c])

    for c in range(RAW):
        at = part_of(c)
        forward(0, c)
        go_right(bot.at[0, at], lb.at[at], lb_s.at[c], lb_r.at[c])
        go_left(top.at[0, at], rt.at[at], rt_s.at[c], rt_r.at[c])
        stay_first(bot.at[0, at], lb.at[at], lb_r.at[c])
        stay_last(top.at[0, at], rt.at[at], rt_r.at[c])

    sum_first()

    for r in range(ROUNDS):
        if r == 0:
            g_tb = jnp.concatenate([sum0[0, H:W], sum0[1, H:W]], axis=0)
            both = jnp.concatenate([sum0[0, 0:H], sum0[1, 0:H]], axis=0)
            both_t = both.T
            ends = jnp.broadcast_to(sum0[0, W : W + 1], (W, W))
            g_tt = jnp.where(row <= col, both, both_t)
            g_bb = jnp.where(row > col, both, jnp.where(row < col, both_t, ends))
        else:
            for copy in shares:
                copy.wait_recv()
                finish.append(copy.wait_send)
            g_tt, g_bb, g_tb = gt[r - 1], gb[r - 1], cross[r - 1]
        for k, value in enumerate((g_tt, g_tb, g_tb.T, g_bb)):
            gram[0, k, INNER] = value

        flag = jnp.broadcast_to(flips_ref[:, r : r + 1], (8, W)) == 1
        swap = jnp.logical_xor(flag, jnp.broadcast_to(p, (8, W)) == 0)
        picked = pick_start(gram.at[0])
        for h in range(2):

            def two(i, carry):
                now, carry = gram_step(gram.at[0], gram.at[1], carry)
                msg[r, h, pl.ds(2 * i, 1)] = now
                now, carry = gram_step(gram.at[1], gram.at[0], carry)
                msg[r, h, pl.ds(2 * i + 1, 1)] = now
                return carry

            picked = lax.fori_loop(0, PART // 2, two, picked)
            msg[r, h, PART:] = jnp.where(swap[:PART], 1.0, 0.0)
            go_right(msg.at[r, h], lmsg.at[r, h], ml_s.at[r, h], ml_r.at[r, h])
            go_left(msg.at[r, h], rmsg.at[r, h], mr_s.at[r, h], mr_r.at[r, h])
            stay_first(msg.at[r, h], lmsg.at[r, h], ml_r.at[r, h])
            stay_last(msg.at[r, h], rmsg.at[r, h], mr_r.at[r, h])
        if r > 0:
            for c in range(CHUNKS - HELD, CHUNKS):
                forward(r, c)

        if r < ROUNDS - 1:
            swaps = jnp.broadcast_to(msg[r, 0, PART : PART + 1], (W, W)) > 0.5
            u, v = gram[0, 0, INNER], gram[0, 3, INNER]
            gx[r] = jnp.where(swaps, v, u)
            gy[r] = jnp.where(swaps, u, v)
            go_right(gx.at[r, mine], gt.at[r, mine], gx_s.at[r], gt_r.at[r])
            go_left(gy.at[r, mine], gb.at[r, mine], gy_s.at[r], gb_r.at[r])
            stay_last(gx.at[r, mine], gb.at[r, mine], gb_r.at[r])
            stay_first(gy.at[r, mine], gt.at[r, mine], gt_r.at[r])

        final = r == ROUNDS - 1
        identity([base, base_l, base_r])
        if not final:
            for h in range(2):
                rebuild([msg.at[r, h]], [base])
            turn = stacked(jnp.concatenate(halves(msg.at[r, 0], base), axis=0))
            for c in [*range(RAW, CHUNKS), *range(RAW)]:
                at = rows_of(c)
                new = times(top[r, at], bot[r, at], turn)
                xs[r, at] = new[:, :W]
                ys[r, at] = new[:, W:]
                if r == 0 and c >= RAW:
                    src = part_of(c)
                    go_right(xs.at[r, src], top.at[1, src], x_s.at[c], x_r.at[c])
                    go_left(ys.at[r, src], bot.at[1, src], y_s.at[c], y_r.at[c])
                    stay_first(ys.at[r, src], top.at[1, src], x_r.at[c])
                    stay_last(xs.at[r, src], bot.at[1, src], y_r.at[c])

        raw = range(RAW if r == 0 else CHUNKS)
        late = [c for c in raw if r > 0 and c >= CHUNKS - HELD]

        def wait_raw(c):
            ref = part_of(c)
            arrived(ft.at[r, ref], ft_r.at[r, c])
            arrived(fb.at[r, ref], fb_r.at[r, c])
            if r == 0:
                arrived(lb.at[ref], lb_r.at[c])
                arrived(rt.at[ref], rt_r.at[c])

        def sides(c):
            at = rows_of(c)
            if r == 0:
                l_b, r_t = lb[at], rt[at]
            else:
                l_b = jnp.where(jnp.broadcast_to(p, (sizes[c], W)) == 0, bot[r, at], ys[r - 1, at])
                r_t = jnp.where(jnp.broadcast_to(p, (sizes[c], W)) == last, top[r, at], xs[r - 1, at])
            return jnp.concatenate([ft[r, at], l_b], axis=1), jnp.concatenate([r_t, fb[r, at]], axis=1)

        def add_sides(c):
            wait_raw(c)
            now = side_gram(*sides(c))
            mid[...] = now if c == 0 else mid[...] + now

        def make(c):
            at, ref = rows_of(c), part_of(c)
            l_pair, r_pair = sides(c)
            news = times(l_pair[:, :W], l_pair[:, W:], turn_l), times(r_pair[:, :W], r_pair[:, W:], turn_r)
            if not final:
                top[r + 1, at], bot[r + 1, at] = news
                if c < CHUNKS - HELD:
                    forward(r + 1, c)
                return
            for h, new in enumerate(news):
                done[h, at] = new
                copy = pltpu.make_async_copy(done.at[h, ref], out.at[ref, pl.ds(h * W, W)], out_sem.at[c, h])
                copy.start()
                finish.append(copy.wait)

        for c in raw:
            if c not in late:
                if final:
                    wait_raw(c)
                else:
                    add_sides(c)

        if final:
            for wait in finish:
                wait()
            finish.clear()
        for h in range(2):
            arrived(lmsg.at[r, h], ml_r.at[r, h])
            arrived(rmsg.at[r, h], mr_r.at[r, h])
            rebuild([lmsg.at[r, h], rmsg.at[r, h]], [base_l, base_r])
        goes, stays = halves(lmsg.at[r, 0], base_l)
        turn_l = stacked(jnp.where(jnp.broadcast_to(p, goes.shape) == 0, stays, goes))
        stays, goes = halves(rmsg.at[r, 0], base_r)
        turn_r = stacked(jnp.where(jnp.broadcast_to(p, goes.shape) == last, stays, goes))

        if final:
            for c in raw:
                if c in late:
                    wait_raw(c)
                make(c)
            continue

        old = list(finish)
        finish.clear()
        make(0)
        for c in late:
            add_sides(c)
        total = turned_gram(turn_l, mid[...], turn_r)
        if r == 0:
            for c in range(RAW, CHUNKS):
                at, ref = rows_of(c), part_of(c)
                arrived(top.at[1, ref], x_r.at[c])
                arrived(bot.at[1, ref], y_r.at[c])
                total = total + cross_gram(top[1, at], bot[1, at])
        part[r] = total

        def between():
            if r == 0:
                for c in range(RAW, CHUNKS - HELD):
                    forward(1, c)
            else:
                make(1)

        shares = [
            remote(buf.at[r, mine], buf.at[r, mine], sg_s.at[r, k], sg_r.at[r, k], sibling)
            for k, buf in enumerate((gt, gb))
        ]

        def during():
            arrived(gt.at[r, mine], gt_r.at[r])
            arrived(gb.at[r, mine], gb_r.at[r])
            for copy in shares:
                copy.start()
            if r > 0:
                for c in range(2, CHUNKS):
                    make(c)
            for wait in old:
                wait()

        sum_small(r, between, during)

    for wait in finish:
        wait()


def body(matrix, flips):
    rows = matrix.shape[0]
    n = lax.axis_size("row")
    R = ROUNDS
    C = CHUNKS
    dma = pltpu.SemaphoreType.DMA

    def vmem(*shape):
        return pltpu.VMEM(shape, F32)

    return pl.pallas_call(
        kernel,
        out_shape=jax.ShapeDtypeStruct(matrix.shape, F32),
        in_specs=[pl.BlockSpec(memory_space=pl.ANY), pl.BlockSpec(memory_space=pltpu.VMEM)],
        out_specs=pl.BlockSpec(memory_space=pl.ANY),
        scratch_shapes=[
            vmem(2, rows, W),
            *(vmem(R, rows, W) for _ in range(6)),
            *(vmem(rows, W) for _ in range(2)),
            *(vmem(2, 4, W + 2 * PAD, W) for _ in range(4)),
            vmem(2 * W, 2 * W),
            vmem(2, W + 8, W),
            vmem(W + 8, W),
            vmem(n // 2, W + 8, W),
            vmem(2, W + 8, W),
            vmem(R - 1, W, W),
            vmem(R - 1, W, W),
            vmem(R - 1, n // 2, W, W),
            vmem(R - 1, W, W),
            *(vmem(R, 2, 2 * PART, W) for _ in range(3)),
            *(vmem(R - 1, W, W) for _ in range(4)),
            dma((C, 2)),
            dma((C, 2)),
            *(dma((R, C)) for _ in range(4)),
            *(dma((C,)) for _ in range(8)),
            *(dma((R, 2)) for _ in range(4)),
            *(dma((R,)) for _ in range(4)),
            dma((2,)),
            dma((2,)),
            dma((n // 2,)),
            dma((n // 2,)),
            dma((R,)),
            dma((R,)),
            dma((R, n // 2)),
            dma((R, n // 2)),
            dma((R, 2)),
            dma((R, 2)),
        ],
        compiler_params=pltpu.CompilerParams(
            collective_id=0, has_side_effects=True, vmem_limit_bytes=46 * 1024 * 1024),
    )(matrix, flips.T)


def solution(mesh):
    placed = (P("row", "col"), P(None, "col"))
    return jax.shard_map(
        body, mesh=mesh, in_specs=placed, out_specs=P("row", "col"), check_vma=False
    )
```
